32 devices in a mesh: tm: 2 (over core), sx: 4 (over y, x), sy: 4 (over z).
Axes of the slice: x: 2, y: 2, z: 4, core: 2. Of those that a mesh axis runs over, the one named last changes fastest.
Arguments:
- slices_state: float32 [2, 64, 16, 16, 128], P('tm', None, 'sx', 'sy'), may hold values from -6 to 6
- forcing: float32 [2, 64, 16, 16, 128], P('tm', None, 'sx', 'sy'), may hold values from -0.6 to 0.6
- initial: float32 [64, 16, 16, 128], P(None, 'sx', 'sy'), may hold values from -6 to 6
- volume: float32 [64, 64], replicated, may hold values from -0.06 to 0.06
- lift: float32 [6, 64, 16], replicated, may hold values from -0.024 to 0.024
Outputs:
- corrected: float32 [2, 64, 16, 16, 128], P('tm', None, 'sx', 'sy')
- residual: float32 [2, 64, 16, 16, 128], P('tm', None, 'sx', 'sy')
The draws below stay inside these ranges and needn't reach their ends.
All inputs are finite; a program needn't handle non-finite values.
Results may differ from the reference program's by a relative error of at most 0.00018.
Values sent between devices are 32-bit elements; how exact they have to be, the bound alone decides.
A program may use at most 64 MiB of HBM per device.

```python
import jax
import jax.numpy as jnp
from jax import lax

DOFS = 64
EZ = 128
SLICES = 2
NEX = 16
NEY = 16


def level_of(rng, dims, cuts, low, high):
    def one(dim, parts):
        draws = jax.random.uniform(jax.random.fold_in(jax.random.fold_in(rng, 6), dim), (parts,), jnp.float32, low / len(cuts), high / len(cuts))
        return jnp.repeat(jnp.exp(draws), dims[dim] // parts).reshape((-1,) + (1,) * (len(dims) - dim - 1))

    factor_of = one(*cuts[0])
    for cut in cuts[1:]:
        factor_of = factor_of * one(*cut)
    return factor_of


def normal_values(key, shape, scale, limit, shards=(), kind=jnp.bfloat16):
    drawn = scale * jax.random.normal(key, shape, jnp.float32)
    if shards:
        drawn = drawn * level_of(key, shape, shards, -0.22, 0.18)
    return jnp.clip(drawn, -limit, limit).astype(kind)


def setup_inputs(seed: int = 0) -> dict:
    key_of = jax.random.split(jax.random.key(seed), 6)
    return {
        "slices_state": normal_values(key_of[0], (SLICES, DOFS, NEX, NEY, EZ), 1.0, 6.0, ((0, 2), (2, 4), (3, 4)), jnp.float32),
        "forcing": normal_values(key_of[1], (SLICES, DOFS, NEX, NEY, EZ), 0.1, 0.6, ((0, 2), (2, 4), (3, 4)), jnp.float32),
        "initial": normal_values(key_of[2], (DOFS, NEX, NEY, EZ), 1.0, 6.0, ((1, 4), (2, 4)), jnp.float32),
        "volume": normal_values(key_of[3], (DOFS, DOFS), 0.01, 0.06, (), jnp.float32),
        "lift": normal_values(key_of[4], (6, DOFS, 16), 0.004, 0.024, (), jnp.float32),
    }


def lower_side(t, axis):
    count = t.shape[axis]
    zero = jnp.zeros_like(lax.slice_in_dim(t, 0, 1, axis=axis))
    return jnp.concatenate([zero, lax.slice_in_dim(t, 0, count - 1, axis=axis)], axis)


def upper_side(t, axis):
    count = t.shape[axis]
    zero = jnp.zeros_like(lax.slice_in_dim(t, 0, 1, axis=axis))
    return jnp.concatenate([lax.slice_in_dim(t, 1, count, axis=axis), zero], axis)


def delta(field, weight, lift_flat):
    width, nx, ny, nz = field.shape
    cube = field.reshape(4, 4, 4, nx, ny, nz)
    x_plus = cube[3].reshape(16, nx, ny, nz)
    x_minus = cube[0].reshape(16, nx, ny, nz)
    y_plus = cube[:, 3].reshape(16, nx, ny, nz)
    y_minus = cube[:, 0].reshape(16, nx, ny, nz)
    z_plus = cube[:, :, 3].reshape(16, nx, ny, nz)
    z_minus = cube[:, :, 0].reshape(16, nx, ny, nz)
    stacked = jnp.concatenate([lower_side(x_plus, 1), upper_side(x_minus, 1), lower_side(y_plus, 2), upper_side(y_minus, 2), lower_side(z_plus, 3), upper_side(z_minus, 3)], 0).reshape(96, -1)
    own = jnp.dot(weight, field.reshape(width, -1), precision=lax.Precision.HIGHEST, preferred_element_type=jnp.float32)
    faces = jnp.dot(lift_flat, stacked, precision=lax.Precision.HIGHEST, preferred_element_type=jnp.float32)
    return (own + faces).reshape(field.shape)


def reference(slices_state, forcing, initial, volume, lift):
    weight = volume - 0.1 * jnp.eye(volume.shape[0], dtype=jnp.float32)
    lift_flat = jnp.transpose(lift, (1, 0, 2)).reshape(volume.shape[0], 96)
    many = jax.vmap(lambda v: delta(v, weight, lift_flat))
    starts = jnp.concatenate([initial[None], slices_state[:-1]], 0)
    relaxed = starts
    for step in range(3):
        relaxed = relaxed + many(relaxed) + forcing
    residual = (relaxed + many(relaxed) + forcing) - slices_state

    def advance(carry, resid_slice):
        nxt = carry + 4.0 * delta(carry, weight, lift_flat) + resid_slice
        return nxt, nxt

    _, error = lax.scan(advance, jnp.zeros_like(initial), residual)
    corrected = slices_state + error
    return corrected, residual
```

```python
import functools

import jax
import jax.numpy as jnp
from jax import lax
from jax.experimental import pallas as pl
from jax.experimental.pallas import tpu as pltpu
from jax.sharding import PartitionSpec as P

MESH = pl.DeviceIdType.MESH
F32, BF16 = jnp.float32, jnp.bfloat16
STEPS = 4
LANES = 128


def halves(value):
    high = value.astype(BF16)
    return high, (value - high.astype(F32)).astype(BF16)


def kernel(
    counts, nx, ny,
    state_hbm, force_hbm, init_hbm, vol_ref, lift_ref,
    corr_hbm, resid_hbm,
    raw_start, raw_state, raw_force, out_c, out_r,
    fields, kept, resid, error, earlier,
    halo_x, halo_y, sent_y, s_high, s_low,
    load_sem, face_send, face_recv, start_send, start_recv, err_send, err_recv, out_sem,
):
    n_tm, n_sx, n_sy = counts
    cells = nx * ny
    tm, sx, sy = lax.axis_index("tm"), lax.axis_index("sx"), lax.axis_index("sy")
    first, more = tm == 0, tm < n_tm - 1
    exists = (sx < n_sx - 1, sx > 0, sy < n_sy - 1, sy > 0)
    comes = (sx > 0, sx < n_sx - 1, sy > 0, sy < n_sy - 1)
    shifts = ((1, 0), (-1, 0), (0, 1), (0, -1))

    def place(dt, f):
        dx, dy = shifts[f]
        return {"tm": tm + dt, "sx": sx + dx, "sy": sy + dy}

    load_state = pltpu.make_async_copy(state_hbm, raw_state, load_sem.at[0])
    load_force = pltpu.make_async_copy(force_hbm, raw_force, load_sem.at[1])
    load_init = pltpu.make_async_copy(init_hbm, raw_start, load_sem.at[2])

    @pl.when(first)
    def _():
        load_init.start()

    load_state.start()
    load_force.start()

    barrier = pltpu.get_barrier_semaphore()

    def greet(dt, f):
        pl.semaphore_signal(barrier, inc=1, device_id=place(dt, f), device_id_type=MESH)

    for f in range(4):
        pl.when(exists[f])(functools.partial(greet, 0, f))
        pl.when(exists[f] & (tm > 0))(functools.partial(greet, -1, f))

    @pl.when(tm > 0)
    def _():
        pl.semaphore_signal(
            barrier, inc=1, device_id={"tm": tm - 1, "sx": sx, "sy": sy}, device_id_type=MESH
        )

    row = lax.broadcasted_iota(jnp.int32, (64, 64), 0)
    column = lax.broadcasted_iota(jnp.int32, (64, 64), 1)
    weight = vol_ref[...] - jnp.where(row == column, 0.1, 0.0).astype(F32)
    matrix = jnp.concatenate([weight] + [lift_ref[f] for f in range(6)], axis=1)
    a_high, a_low = halves(matrix)
    a_both = jnp.concatenate([a_high, a_low], axis=0)
    face_matrix = []
    for f in range(4):
        high, low = halves(lift_ref[f])
        face_matrix.append(
            jnp.concatenate([high.astype(F32), high.astype(F32), low.astype(F32)], axis=1).astype(BF16)
        )

    wide, tall = ny * LANES, cells * LANES
    for stack in (s_high, s_low):
        stack[64:80, 0:wide] = jnp.zeros((16, wide), BF16)
        stack[80:96, tall - wide : tall] = jnp.zeros((16, wide), BF16)
        for x in range(nx):
            low, high = x * wide, (x + 1) * wide
            stack[96:112, low : low + LANES] = jnp.zeros((16, LANES), BF16)
            stack[112:128, high - LANES : high] = jnp.zeros((16, LANES), BF16)

    def no_halo(f):
        ref = (halo_x, halo_x, halo_y, halo_y)[f]
        for phase in range(STEPS + 1):
            ref[phase, f % 2] = jnp.zeros(ref.shape[2:], F32)

    for f in range(4):
        pl.when(jnp.logical_not(comes[f]))(functools.partial(no_halo, f))

    total = sum(e.astype(jnp.int32) for e in exists)
    pl.semaphore_wait(barrier, total + jnp.where(more, total + 1, 0))

    start_copy = pltpu.make_async_remote_copy(
        src_ref=state_hbm, dst_ref=raw_start, send_sem=start_send, recv_sem=start_recv,
        device_id={"tm": tm + 1, "sx": sx, "sy": sy}, device_id_type=MESH,
    )

    @pl.when(more)
    def _():
        start_copy.start()

    top = lax.broadcasted_iota(jnp.int32, (8, LANES), 0) < 4
    lane = lax.broadcasted_iota(jnp.int32, (16, LANES), 1)

    def y_plus(ref, cell):
        parts = []
        for p in range(0, 64, 32):
            one, two = ref[cell, p + 8 : p + 16, :], ref[cell, p + 24 : p + 32, :]
            parts.append(jnp.where(top, pltpu.roll(one, 4, 0), two))
        return jnp.concatenate(parts, axis=0)

    def y_minus(ref, cell):
        parts = []
        for p in range(0, 64, 32):
            one, two = ref[cell, p : p + 8, :], ref[cell, p + 16 : p + 24, :]
            parts.append(jnp.where(top, one, pltpu.roll(two, 4, 0)))
        return jnp.concatenate(parts, axis=0)

    def face_copy(ref, slot, phase, dt, f, to=None):
        if f == 0:
            src = ref.at[pl.ds(cells - ny, ny), pl.ds(48, 16), :]
        elif f == 1:
            src = ref.at[pl.ds(0, ny), pl.ds(0, 16), :]
        else:
            src = sent_y.at[slot, f - 2]
        target = (halo_x, halo_x, halo_y, halo_y)[f].at[phase, f % 2]
        return pltpu.make_async_remote_copy(
            src_ref=src, dst_ref=target,
            send_sem=face_send.at[slot, f], recv_sem=face_recv.at[phase, f],
            device_id=place(dt, f if to is None else to), device_id_type=MESH,
        )

    def send_faces(ref, slot, phase, dt):
        for f in range(2):
            pl.when(exists[f])(face_copy(ref, slot, phase, dt, f).start)
        for x in range(nx):
            sent_y[slot, 0, x] = y_plus(ref, x * ny + ny - 1)
            sent_y[slot, 1, x] = y_minus(ref, x * ny)
        for f in range(2, 4):
            pl.when(exists[f])(face_copy(ref, slot, phase, dt, f).start)

    def sent_faces(ref, slot, phase, dt):
        for f in range(4):
            pl.when(exists[f])(face_copy(ref, slot, phase, dt, f).wait_send)

    def reorder(raw, ref):
        for cell in range(cells):
            ref[cell] = raw[pl.ds(cell, 64, stride=cells), :]

    def inside(ref, finish):
        def put(rows, cell, value):
            high, low = halves(value)
            cols = slice(cell * LANES, (cell + 1) * LANES)
            s_high[rows : rows + value.shape[0], cols] = high
            s_low[rows : rows + value.shape[0], cols] = low

        for x in range(nx):
            for y in range(ny):
                cell = x * ny + y
                put(0, cell, ref[cell])
                if x + 1 < nx:
                    put(64, cell + ny, ref[cell, 48:64, :])
                if x > 0:
                    put(80, cell - ny, ref[cell, 0:16, :])
                if y + 1 < ny:
                    put(96, cell + 1, y_plus(ref, cell))
                if y > 0:
                    put(112, cell - 1, y_minus(ref, cell))
                up = pltpu.roll(ref[cell, pl.ds(3, 16, stride=4), :], 1, 1)
                put(128, cell, jnp.where(lane == 0, 0.0, up))
                down = pltpu.roll(ref[cell, pl.ds(0, 16, stride=4), :], LANES - 1, 1)
                put(144, cell, jnp.where(lane == LANES - 1, 0.0, down))
        for x in range(nx):
            cols = slice(x * wide, (x + 1) * wide)
            both = jnp.dot(a_both, s_high[:, cols], preferred_element_type=F32)
            rest = jnp.dot(a_high, s_low[:, cols], preferred_element_type=F32)
            delta = both[:64] + both[64:] + rest
            for y in range(ny):
                finish(x * ny + y, delta[:, y * LANES : (y + 1) * LANES])

    def outside(phase, out, scale):
        for f in range(4):
            pl.when(comes[f])(face_copy(kept, STEPS + 1, phase, 0, f, f ^ 1).wait_recv)
        for f in range(4):
            ref = (halo_x, halo_x, halo_y, halo_y)[f]
            count = ref.shape[2]
            trace = jnp.concatenate([ref[phase, f % 2, i] for i in range(count)], axis=1)
            high, low = halves(trace)
            added = jnp.dot(
                face_matrix[f], jnp.concatenate([high, low, high], axis=0), preferred_element_type=F32
            )
            if scale != 1.0:
                added = scale * added
            for i in range(count):
                cell = (i, cells - ny + i, i * ny, i * ny + ny - 1)[f]
                out[cell] = out[cell] + added[:, i * LANES : (i + 1) * LANES]

    @pl.when(first)
    def _():
        load_init.wait()
        reorder(raw_start, fields.at[0])
        send_faces(fields.at[0], 0, 0, 0)

    load_state.wait()
    reorder(raw_state, kept)

    @pl.when(more)
    def _():
        send_faces(kept, STEPS + 1, 0, 1)

    load_force.wait()

    @pl.when(jnp.logical_not(first))
    def _():
        start_copy.wait_recv()
        reorder(raw_start, fields.at[0])

    for step in range(STEPS):
        now = fields.at[step]
        last = step == STEPS - 1
        out = resid if last else fields.at[step + 1]
        if step > 0:
            send_faces(now, step, step, 0)

        def finish(cell, delta, now=now, out=out, last=last):
            value = now[cell] + delta + raw_force[pl.ds(cell, 64, stride=cells), :]
            out[cell] = value - kept[cell] if last else value

        inside(now, finish)
        outside(step, out, 1.0)

    def err_copy(x):
        part = pl.ds(x * ny, ny)
        return pltpu.make_async_remote_copy(
            src_ref=error.at[part], dst_ref=earlier.at[part],
            send_sem=err_send.at[x], recv_sem=err_recv.at[x],
            device_id={"tm": tm + 1, "sx": sx, "sy": sy}, device_id_type=MESH,
        )

    @pl.when(first)
    def _():
        for cell in range(cells):
            error[cell] = resid[cell]

    def store_resid():
        for cell in range(cells):
            out_r[pl.ds(cell, 64, stride=cells), :] = resid[cell]
        pltpu.make_async_copy(out_r, resid_hbm, out_sem.at[0]).start()

    @pl.when(jnp.logical_not(first))
    def _():
        store_resid()
        for x in range(nx):
            err_copy(x).wait_recv()

        def finish(cell, delta):
            error[cell] = resid[cell] + earlier[cell] + 4.0 * delta

        inside(earlier, finish)
        outside(STEPS, error, 4.0)

    @pl.when(more)
    def _():
        for x in range(nx):
            err_copy(x).start()
        send_faces(error, STEPS, STEPS, 1)

    pl.when(first)(store_resid)
    for cell in range(cells):
        out_c[pl.ds(cell, 64, stride=cells), :] = kept[cell] + error[cell]
    store = pltpu.make_async_copy(out_c, corr_hbm, out_sem.at[1])
    store.start()

    @pl.when(first)
    def _():
        sent_faces(fields.at[0], 0, 0, 0)

    for step in range(1, STEPS):
        sent_faces(fields.at[step], step, step, 0)

    @pl.when(more)
    def _():
        start_copy.wait_send()
        sent_faces(kept, STEPS + 1, 0, 1)
        for x in range(nx):
            err_copy(x).wait_send()
        sent_faces(error, STEPS, STEPS, 1)

    pltpu.make_async_copy(out_r, resid_hbm, out_sem.at[0]).wait()
    store.wait()


def solution(mesh):
    counts = tuple(mesh.shape[axis] for axis in ("tm", "sx", "sy"))

    def local(slices_state, forcing, initial, volume, lift):
        _, dofs, nx, ny, nz = slices_state.shape
        cells = nx * ny
        rows = dofs * cells
        raw = pltpu.VMEM((rows, nz), F32)
        field = pltpu.VMEM((cells, dofs, nz), F32)
        stack = pltpu.VMEM((160, cells * nz), BF16)
        flat = jax.ShapeDtypeStruct((rows, nz), F32)
        corrected, residual = pl.pallas_call(
            functools.partial(kernel, counts, nx, ny),
            out_shape=(flat, flat),
            in_specs=[pl.BlockSpec(memory_space=pl.ANY)] * 3
            + [pl.BlockSpec(memory_space=pltpu.VMEM)] * 2,
            out_specs=(pl.BlockSpec(memory_space=pl.ANY),) * 2,
            scratch_shapes=[
                raw, raw, raw, raw, raw,
                pltpu.VMEM((STEPS, cells, dofs, nz), F32), field, field, field, field,
                pltpu.VMEM((STEPS + 1, 2, ny, 16, nz), F32),
                pltpu.VMEM((STEPS + 1, 2, nx, 16, nz), F32),
                pltpu.VMEM((STEPS + 2, 2, nx, 16, nz), F32),
                stack, stack,
                pltpu.SemaphoreType.DMA((3,)),
                pltpu.SemaphoreType.DMA((STEPS + 2, 4)),
                pltpu.SemaphoreType.DMA((STEPS + 1, 4)),
                pltpu.SemaphoreType.DMA,
                pltpu.SemaphoreType.DMA,
                pltpu.SemaphoreType.DMA((nx,)),
                pltpu.SemaphoreType.DMA((nx,)),
                pltpu.SemaphoreType.DMA((2,)),
            ],
            compiler_params=pltpu.CompilerParams(
                collective_id=0, has_side_effects=True, vmem_limit_bytes=32 * 2**20
            ),
            name="cycle",
        )(
            slices_state.reshape(rows, nz), forcing.reshape(rows, nz), initial.reshape(rows, nz),
            volume, lift,
        )
        shape = slices_state.shape
        return corrected.reshape(shape), residual.reshape(shape)

    split = P("tm", None, "sx", "sy", None)
    return jax.shard_map(
        local,
        mesh=mesh,
        in_specs=(split, split, P(None, "sx", "sy", None), P(), P()),
        out_specs=(split, split),
        check_vma=False,
    )
```

```python
import functools

import jax
import jax.numpy as jnp
from jax import lax
from jax.experimental import pallas as pl
from jax.experimental.pallas import tpu as pltpu
from jax.sharding import PartitionSpec as P

MESH = pl.DeviceIdType.MESH
F32, BF16 = jnp.float32, jnp.bfloat16
STEPS = 4
LANES = 128


def halves(value):
    high = value.astype(BF16)
    return high, (value - high.astype(F32)).astype(BF16)


def kernel(
    counts, nx, ny,
    state_hbm, force_hbm, init_hbm, vol_hbm, lift_hbm,
    kept, resid, error,
    raw_start, raw_state, raw_force, volume, lift,
    fields, source, earlier,
    halo_x, halo_y, sent_y, s_high, s_low,
    load_sem, face_send, face_recv, start_send, start_recv, err_send, err_recv,
):
    n_tm, n_sx, n_sy = counts
    cells = nx * ny
    tm, sx, sy = lax.axis_index("tm"), lax.axis_index("sx"), lax.axis_index("sy")
    first, more = tm == 0, tm < n_tm - 1
    exists = (sx < n_sx - 1, sx > 0, sy < n_sy - 1, sy > 0)
    comes = (sx > 0, sx < n_sx - 1, sy > 0, sy < n_sy - 1)
    shifts = ((1, 0), (-1, 0), (0, 1), (0, -1))

    def place(dt, f):
        dx, dy = shifts[f]
        return {"tm": tm + dt, "sx": sx + dx, "sy": sy + dy}

    load_state = pltpu.make_async_copy(state_hbm, raw_state, load_sem.at[0])
    load_force = pltpu.make_async_copy(force_hbm, raw_force, load_sem.at[1])
    load_init = pltpu.make_async_copy(init_hbm, raw_start, load_sem.at[2])

    @pl.when(first)
    def _():
        load_init.start()

    load_state.start()
    load_force.start()
    load_volume = pltpu.make_async_copy(vol_hbm, volume, load_sem.at[3])
    load_lift = pltpu.make_async_copy(lift_hbm, lift, load_sem.at[4])
    load_volume.start()
    load_lift.start()

    barrier = pltpu.get_barrier_semaphore()

    def greet(dt, f):
        pl.semaphore_signal(barrier, inc=1, device_id=place(dt, f), device_id_type=MESH)

    for f in range(4):
        pl.when(exists[f])(functools.partial(greet, 0, f))
        pl.when(exists[f] & (tm > 0))(functools.partial(greet, -1, f))

    @pl.when(tm > 0)
    def _():
        pl.semaphore_signal(
            barrier, inc=1, device_id={"tm": tm - 1, "sx": sx, "sy": sy}, device_id_type=MESH
        )

    wide, tall = ny * LANES, cells * LANES
    for stack in (s_high, s_low):
        stack[64:80, 0:wide] = jnp.zeros((16, wide), BF16)
        stack[80:96, tall - wide : tall] = jnp.zeros((16, wide), BF16)
        for x in range(nx):
            low, high = x * wide, (x + 1) * wide
            stack[96:112, low : low + LANES] = jnp.zeros((16, LANES), BF16)
            stack[112:128, high - LANES : high] = jnp.zeros((16, LANES), BF16)

    def no_halo(f):
        ref = (halo_x, halo_x, halo_y, halo_y)[f]
        for phase in range(STEPS + 1):
            ref[phase, f % 2] = jnp.zeros(ref.shape[2:], F32)

    for f in range(4):
        pl.when(jnp.logical_not(comes[f]))(functools.partial(no_halo, f))

    total = sum(e.astype(jnp.int32) for e in exists)
    pl.semaphore_wait(barrier, total + jnp.where(more, total + 1, 0))

    def start_copy(x):
        part = pl.ds(x * 64 * ny, 64 * ny)
        return pltpu.make_async_remote_copy(
            src_ref=state_hbm.at[part], dst_ref=raw_start.at[part],
            send_sem=start_send.at[x], recv_sem=start_recv.at[x],
            device_id={"tm": tm + 1, "sx": sx, "sy": sy}, device_id_type=MESH,
        )

    @pl.when(more)
    def _():
        for x in range(nx):
            start_copy(x).start()

    top = lax.broadcasted_iota(jnp.int32, (8, LANES), 0) < 4
    lane = lax.broadcasted_iota(jnp.int32, (16, LANES), 1)

    def y_plus(ref, cell):
        parts = []
        for p in range(0, 64, 32):
            one, two = ref[cell, p + 8 : p + 16, :], ref[cell, p + 24 : p + 32, :]
            parts.append(jnp.where(top, pltpu.roll(one, 4, 0), two))
        return jnp.concatenate(parts, axis=0)

    def y_minus(ref, cell):
        parts = []
        for p in range(0, 64, 32):
            one, two = ref[cell, p : p + 8, :], ref[cell, p + 16 : p + 24, :]
            parts.append(jnp.where(top, one, pltpu.roll(two, 4, 0)))
        return jnp.concatenate(parts, axis=0)

    def face_copy(ref, slot, phase, dt, f, to=None):
        if f == 0:
            src = ref.at[pl.ds(cells - ny, ny), pl.ds(48, 16), :]
        elif f == 1:
            src = ref.at[pl.ds(0, ny), pl.ds(0, 16), :]
        else:
            src = sent_y.at[slot, f - 2]
        target = (halo_x, halo_x, halo_y, halo_y)[f].at[phase, f % 2]
        return pltpu.make_async_remote_copy(
            src_ref=src, dst_ref=target,
            send_sem=face_send.at[slot, f], recv_sem=face_recv.at[phase, f],
            device_id=place(dt, f if to is None else to), device_id_type=MESH,
        )

    def send_faces(ref, slot, phase, dt):
        for f in range(2):
            pl.when(exists[f])(face_copy(ref, slot, phase, dt, f).start)
        for x in range(nx):
            sent_y[slot, 0, x] = y_plus(ref, x * ny + ny - 1)
            sent_y[slot, 1, x] = y_minus(ref, x * ny)
        for f in range(2, 4):
            pl.when(exists[f])(face_copy(ref, slot, phase, dt, f).start)

    def sent_faces(ref, slot, phase, dt):
        for f in range(4):
            pl.when(exists[f])(face_copy(ref, slot, phase, dt, f).wait_send)

    def reorder(raw, ref):
        for cell in range(cells):
            ref[cell] = raw[pl.ds(cell, 64, stride=cells), :]

    def inside(ref, finish):
        def put(rows, cell, value):
            high, low = halves(value)
            cols = slice(cell * LANES, (cell + 1) * LANES)
            s_high[rows : rows + value.shape[0], cols] = high
            s_low[rows : rows + value.shape[0], cols] = low

        for x in range(nx):
            for y in range(ny):
                cell = x * ny + y
                pair = halves(ref[cell])
                for stack, half in zip((s_high, s_low), pair):
                    stack[0:64, cell * LANES : (cell + 1) * LANES] = half
                    if x + 1 < nx:
                        stack[64:80, (cell + ny) * LANES : (cell + ny + 1) * LANES] = half[48:64]
                    if x > 0:
                        stack[80:96, (cell - ny) * LANES : (cell - ny + 1) * LANES] = half[0:16]
                if y + 1 < ny:
                    put(96, cell + 1, y_plus(ref, cell))
                if y > 0:
                    put(112, cell - 1, y_minus(ref, cell))
                up = pltpu.roll(ref[cell, pl.ds(3, 16, stride=4), :], 1, 1)
                put(128, cell, jnp.where(lane == 0, 0.0, up))
                down = pltpu.roll(ref[cell, pl.ds(0, 16, stride=4), :], LANES - 1, 1)
                put(144, cell, jnp.where(lane == LANES - 1, 0.0, down))
        for x in range(nx):
            cols = slice(x * wide, (x + 1) * wide)
            both = jnp.dot(a_both, s_high[:, cols], preferred_element_type=F32)
            rest = jnp.dot(a_high, s_low[:, cols], preferred_element_type=F32)
            delta = both[:64] + both[64:] + rest
            for y in range(ny):
                finish(x * ny + y, delta[:, y * LANES : (y + 1) * LANES])

    def outside(phase, out, scale):
        for f in range(4):
            pl.when(comes[f])(face_copy(kept, STEPS + 1, phase, 0, f, f ^ 1).wait_recv)
        for f in range(4):
            ref = (halo_x, halo_x, halo_y, halo_y)[f]
            count = ref.shape[2]
            trace = jnp.concatenate([ref[phase, f % 2, i] for i in range(count)], axis=1)
            high, low = halves(trace)
            added = jnp.dot(
                face_matrix[f], jnp.concatenate([high, low, high], axis=0), preferred_element_type=F32
            )
            if scale != 1.0:
                added = scale * added
            for i in range(count):
                cell = (i, cells - ny + i, i * ny, i * ny + ny - 1)[f]
                out[cell] = out[cell] + added[:, i * LANES : (i + 1) * LANES]

    @pl.when(first)
    def _():
        load_init.wait()
        reorder(raw_start, fields.at[0])
        send_faces(fields.at[0], 0, 0, 0)

    load_state.wait()
    reorder(raw_state, kept)

    @pl.when(more)
    def _():
        send_faces(kept, STEPS + 1, 0, 1)

    load_force.wait()
    reorder(raw_force, source)

    load_volume.wait()
    load_lift.wait()
    row = lax.broadcasted_iota(jnp.int32, (64, 64), 0)
    column = lax.broadcasted_iota(jnp.int32, (64, 64), 1)
    weight = volume[...] - jnp.where(row == column, 0.1, 0.0).astype(F32)
    lifts = jnp.concatenate([lift[f] for f in range(6)], axis=0).T
    a_high, a_low = halves(jnp.concatenate([weight, lifts], axis=1))
    a_both = jnp.concatenate([a_high, a_low], axis=0)
    face_matrix = []
    for f in range(4):
        high, low = halves(lifts[:, 16 * f : 16 * f + 16])
        face_matrix.append(
            jnp.concatenate([high.astype(F32), high.astype(F32), low.astype(F32)], axis=1).astype(BF16)
        )

    @pl.when(jnp.logical_not(first))
    def _():
        for x in range(nx):
            start_copy(x).wait_recv()
        reorder(raw_start, fields.at[0])

    for step in range(STEPS):
        now = fields.at[step]
        last = step == STEPS - 1
        out = resid if last else fields.at[step + 1]
        if step > 0:
            send_faces(now, step, step, 0)

        def finish(cell, delta, now=now, out=out, last=last):
            value = now[cell] + delta + source[cell]
            out[cell] = value - kept[cell] if last else value

        inside(now, finish)
        outside(step, out, 1.0)

    def err_copy(x):
        part = pl.ds(x * ny, ny)
        return pltpu.make_async_remote_copy(
            src_ref=error.at[part], dst_ref=earlier.at[part],
            send_sem=err_send.at[x], recv_sem=err_recv.at[x],
            device_id={"tm": tm + 1, "sx": sx, "sy": sy}, device_id_type=MESH,
        )

    @pl.when(first)
    def _():
        for cell in range(cells):
            error[cell] = resid[cell]

    @pl.when(jnp.logical_not(first))
    def _():
        for x in range(nx):
            err_copy(x).wait_recv()

        def finish(cell, delta):
            error[cell] = resid[cell] + earlier[cell] + 4.0 * delta

        inside(earlier, finish)
        outside(STEPS, error, 4.0)

    @pl.when(more)
    def _():
        for x in range(nx):
            err_copy(x).start()
        send_faces(error, STEPS, STEPS, 1)

    @pl.when(first)
    def _():
        sent_faces(fields.at[0], 0, 0, 0)

    for step in range(1, STEPS):
        sent_faces(fields.at[step], step, step, 0)

    @pl.when(more)
    def _():
        sent_faces(kept, STEPS + 1, 0, 1)
        for x in range(nx):
            start_copy(x).wait_send()
            err_copy(x).wait_send()
        sent_faces(error, STEPS, STEPS, 1)


def finishing(nx, ny, kept, resid, error, corr_hbm, resid_hbm, out_c, out_r, out_sem):
    cells = nx * ny
    copies = []
    for part in range(4):
        low, rows = part * 16 * cells, 16 * cells
        for cell in range(cells):
            dofs = slice(part * 16, part * 16 + 16)
            value = resid[cell, dofs, :]
            out_r[pl.ds(low + cell, 16, stride=cells), :] = value
            out_c[pl.ds(low + cell, 16, stride=cells), :] = kept[cell, dofs, :] + error[cell, dofs, :]
        for i, (src, dst) in enumerate(((out_r, resid_hbm), (out_c, corr_hbm))):
            span = pl.ds(low, rows)
            copies.append(pltpu.make_async_copy(src.at[span], dst.at[span], out_sem.at[part, i]))
            copies[-1].start()
    for copy in copies:
        copy.wait()


def solution(mesh):
    counts = tuple(mesh.shape[axis] for axis in ("tm", "sx", "sy"))

    def local(slices_state, forcing, initial, volume, lift):
        _, dofs, nx, ny, nz = slices_state.shape
        cells = nx * ny
        rows = dofs * cells
        raw = pltpu.VMEM((rows, nz), F32)
        field = pltpu.VMEM((cells, dofs, nz), F32)
        stack = pltpu.VMEM((160, cells * nz), BF16)
        flat = jax.ShapeDtypeStruct((rows, nz), F32)
        shaped = jax.ShapeDtypeStruct((cells, dofs, nz), F32)
        vmem, hbm = pl.BlockSpec(memory_space=pltpu.VMEM), pl.BlockSpec(memory_space=pltpu.HBM)
        parts = pl.pallas_call(
            functools.partial(kernel, counts, nx, ny),
            out_shape=(shaped,) * 3,
            in_specs=[hbm] * 5,
            out_specs=(vmem,) * 3,
            scratch_shapes=[
                raw, raw, raw, pltpu.VMEM(volume.shape, F32), pltpu.VMEM((6, 16, dofs), F32),
                pltpu.VMEM((STEPS, cells, dofs, nz), F32), field, field,
                pltpu.VMEM((STEPS + 1, 2, ny, 16, nz), F32),
                pltpu.VMEM((STEPS + 1, 2, nx, 16, nz), F32),
                pltpu.VMEM((STEPS + 2, 2, nx, 16, nz), F32),
                stack, stack,
                pltpu.SemaphoreType.DMA((5,)),
                pltpu.SemaphoreType.DMA((STEPS + 2, 4)),
                pltpu.SemaphoreType.DMA((STEPS + 1, 4)),
                pltpu.SemaphoreType.DMA((nx,)),
                pltpu.SemaphoreType.DMA((nx,)),
                pltpu.SemaphoreType.DMA((nx,)),
                pltpu.SemaphoreType.DMA((nx,)),
            ],
            compiler_params=pltpu.CompilerParams(
                collective_id=0, has_side_effects=True, vmem_limit_bytes=32 * 2**20
            ),
            name="cycle",
        )(
            *(
                pltpu.with_memory_space_constraint(value, pltpu.HBM)
                for value in (
                    slices_state.reshape(rows, nz), forcing.reshape(rows, nz),
                    initial.reshape(rows, nz), volume, jnp.swapaxes(lift, 1, 2),
                )
            )
        )
        corrected, residual = pl.pallas_call(
            functools.partial(finishing, nx, ny),
            out_shape=(flat,) * 2,
            in_specs=[vmem] * 3,
            out_specs=(hbm,) * 2,
            scratch_shapes=[raw, raw, pltpu.SemaphoreType.DMA((4, 2))],
            compiler_params=pltpu.CompilerParams(vmem_limit_bytes=16 * 2**20),
            name="finishing",
        )(*parts)
        shape = slices_state.shape
        return corrected.reshape(shape), residual.reshape(shape)

    split = P("tm", None, "sx", "sy", None)
    return jax.shard_map(
        local,
        mesh=mesh,
        in_specs=(split, split, P(None, "sx", "sy", None), P(), P()),
        out_specs=(split, split),
        check_vma=False,
    )
```

```python
import functools

import jax
import jax.numpy as jnp
from jax import lax
from jax.experimental import pallas as pl
from jax.experimental.pallas import tpu as pltpu
from jax.sharding import PartitionSpec as P

MESH = pl.DeviceIdType.MESH
F32, BF16 = jnp.float32, jnp.bfloat16
STEPS = 4
LANES = 128


def halves(value):
    high = value.astype(BF16)
    return high, (value - high.astype(F32)).astype(BF16)


def kernel(
    counts, nx, ny,
    state_hbm, force_hbm, init_hbm, vol_hbm, lift_hbm,
    kept, resid, error,
    raw_start, raw_state, raw_force, volume, lift,
    fields, source, earlier,
    halo_x, halo_y, sent_y, s_high, s_low,
    load_sem, face_send, face_recv, start_send, start_recv, err_send, err_recv,
):
    n_tm, n_sx, n_sy = counts
    cells = nx * ny
    tm, sx, sy = lax.axis_index("tm"), lax.axis_index("sx"), lax.axis_index("sy")
    first, more = tm == 0, tm < n_tm - 1
    exists = (sx < n_sx - 1, sx > 0, sy < n_sy - 1, sy > 0)
    comes = (sx > 0, sx < n_sx - 1, sy > 0, sy < n_sy - 1)
    shifts = ((1, 0), (-1, 0), (0, 1), (0, -1))

    def place(dt, f):
        dx, dy = shifts[f]
        return {"tm": tm + dt, "sx": sx + dx, "sy": sy + dy}

    load_state = pltpu.make_async_copy(state_hbm, raw_state, load_sem.at[0])
    load_force = pltpu.make_async_copy(force_hbm, raw_force, load_sem.at[1])
    load_init = pltpu.make_async_copy(init_hbm, raw_start, load_sem.at[2])

    @pl.when(first)
    def _():
        load_init.start()

    load_state.start()
    load_force.start()
    load_volume = pltpu.make_async_copy(vol_hbm, volume, load_sem.at[3])
    load_lift = pltpu.make_async_copy(lift_hbm, lift, load_sem.at[4])
    load_volume.start()
    load_lift.start()

    barrier = pltpu.get_barrier_semaphore()

    def greet(dt, f):
        pl.semaphore_signal(barrier, inc=1, device_id=place(dt, f), device_id_type=MESH)

    for f in range(4):
        pl.when(exists[f])(functools.partial(greet, 0, f))
        pl.when(exists[f] & (tm > 0))(functools.partial(greet, -1, f))

    @pl.when(tm > 0)
    def _():
        pl.semaphore_signal(
            barrier, inc=1, device_id={"tm": tm - 1, "sx": sx, "sy": sy}, device_id_type=MESH
        )

    wide, tall = ny * LANES, cells * LANES
    for stack in (s_high, s_low):
        stack[64:80, 0:wide] = jnp.zeros((16, wide), BF16)
        stack[80:96, tall - wide : tall] = jnp.zeros((16, wide), BF16)
        for x in range(nx):
            low, high = x * wide, (x + 1) * wide
            stack[96:112, low : low + LANES] = jnp.zeros((16, LANES), BF16)
            stack[112:128, high - LANES : high] = jnp.zeros((16, LANES), BF16)

    def no_halo(f):
        ref = (halo_x, halo_x, halo_y, halo_y)[f]
        for phase in range(STEPS + 1):
            ref[phase, f % 2] = jnp.zeros(ref.shape[2:], F32)

    for f in range(4):
        pl.when(jnp.logical_not(comes[f]))(functools.partial(no_halo, f))

    total = sum(e.astype(jnp.int32) for e in exists)
    pl.semaphore_wait(barrier, total + jnp.where(more, total + 1, 0))

    def start_copy(x):
        part = pl.ds(x * 64 * ny, 64 * ny)
        return pltpu.make_async_remote_copy(
            src_ref=state_hbm.at[part], dst_ref=raw_start.at[part],
            send_sem=start_send.at[x], recv_sem=start_recv.at[x],
            device_id={"tm": tm + 1, "sx": sx, "sy": sy}, device_id_type=MESH,
        )

    @pl.when(more)
    def _():
        for x in range(nx):
            start_copy(x).start()

    top = lax.broadcasted_iota(jnp.int32, (8, LANES), 0) < 4
    lane = lax.broadcasted_iota(jnp.int32, (16, LANES), 1)

    def y_plus(ref, cell):
        parts = []
        for p in range(0, 64, 32):
            one, two = ref[cell, p + 8 : p + 16, :], ref[cell, p + 24 : p + 32, :]
            parts.append(jnp.where(top, pltpu.roll(one, 4, 0), two))
        return jnp.concatenate(parts, axis=0)

    def y_minus(ref, cell):
        parts = []
        for p in range(0, 64, 32):
            one, two = ref[cell, p : p + 8, :], ref[cell, p + 16 : p + 24, :]
            parts.append(jnp.where(top, one, pltpu.roll(two, 4, 0)))
        return jnp.concatenate(parts, axis=0)

    def face_copy(ref, slot, phase, dt, f, to=None):
        if f == 0:
            src = ref.at[pl.ds(cells - ny, ny), pl.ds(48, 16), :]
        elif f == 1:
            src = ref.at[pl.ds(0, ny), pl.ds(0, 16), :]
        else:
            src = sent_y.at[slot, f - 2]
        target = (halo_x, halo_x, halo_y, halo_y)[f].at[phase, f % 2]
        return pltpu.make_async_remote_copy(
            src_ref=src, dst_ref=target,
            send_sem=face_send.at[slot, f], recv_sem=face_recv.at[phase, f],
            device_id=place(dt, f if to is None else to), device_id_type=MESH,
        )

    def send_faces(ref, slot, phase, dt):
        odd = lax.rem(sx, 2) == 1
        pl.when(exists[0] & odd)(face_copy(ref, slot, phase, dt, 0).start)
        pl.when(exists[1])(face_copy(ref, slot, phase, dt, 1).start)
        pl.when(exists[0] & jnp.logical_not(odd))(face_copy(ref, slot, phase, dt, 0).start)
        for x in range(nx):
            sent_y[slot, 0, x] = y_plus(ref, x * ny + ny - 1)
            sent_y[slot, 1, x] = y_minus(ref, x * ny)
        for f in range(2, 4):
            pl.when(exists[f])(face_copy(ref, slot, phase, dt, f).start)

    def sent_faces(ref, slot, phase, dt):
        for f in range(4):
            pl.when(exists[f])(face_copy(ref, slot, phase, dt, f).wait_send)

    def reorder(raw, ref):
        for cell in range(cells):
            ref[cell] = raw[pl.ds(cell, 64, stride=cells), :]

    def inside(ref, finish):
        def put(rows, cell, value):
            high, low = halves(value)
            cols = slice(cell * LANES, (cell + 1) * LANES)
            s_high[rows : rows + value.shape[0], cols] = high
            s_low[rows : rows + value.shape[0], cols] = low

        for x in range(nx):
            for y in range(ny):
                cell = x * ny + y
                pair = halves(ref[cell])
                for stack, half in zip((s_high, s_low), pair):
                    stack[0:64, cell * LANES : (cell + 1) * LANES] = half
                    if x + 1 < nx:
                        stack[64:80, (cell + ny) * LANES : (cell + ny + 1) * LANES] = half[48:64]
                    if x > 0:
                        stack[80:96, (cell - ny) * LANES : (cell - ny + 1) * LANES] = half[0:16]
                if y + 1 < ny:
                    put(96, cell + 1, y_plus(ref, cell))
                if y > 0:
                    put(112, cell - 1, y_minus(ref, cell))
                up = pltpu.roll(ref[cell, pl.ds(3, 16, stride=4), :], 1, 1)
                put(128, cell, jnp.where(lane == 0, 0.0, up))
                down = pltpu.roll(ref[cell, pl.ds(0, 16, stride=4), :], LANES - 1, 1)
                put(144, cell, jnp.where(lane == LANES - 1, 0.0, down))
        for x in range(nx):
            cols = slice(x * wide, (x + 1) * wide)
            both = jnp.dot(a_both, s_high[:, cols], preferred_element_type=F32)
            rest = jnp.dot(a_high, s_low[:, cols], preferred_element_type=F32)
            delta = both[:64] + both[64:] + rest
            for y in range(ny):
                finish(x * ny + y, delta[:, y * LANES : (y + 1) * LANES])

    def outside(phase, out, scale):
        for faces in ((2, 3), (0, 1)):
            for f in faces:
                pl.when(comes[f])(face_copy(kept, STEPS + 1, phase, 0, f, f ^ 1).wait_recv)
            for f in faces:
                ref = (halo_x, halo_x, halo_y, halo_y)[f]
                count = ref.shape[2]
                trace = jnp.concatenate([ref[phase, f % 2, i] for i in range(count)], axis=1)
                high, low = halves(trace)
                added = jnp.dot(
                    face_matrix[f], jnp.concatenate([high, low, high], axis=0), preferred_element_type=F32
                )
                if scale != 1.0:
                    added = scale * added
                for i in range(count):
                    cell = (i, cells - ny + i, i * ny, i * ny + ny - 1)[f]
                    out[cell] = out[cell] + added[:, i * LANES : (i + 1) * LANES]

    @pl.when(first)
    def _():
        load_init.wait()
        reorder(raw_start, fields.at[0])
        send_faces(fields.at[0], 0, 0, 0)

    load_state.wait()
    reorder(raw_state, kept)

    @pl.when(more)
    def _():
        send_faces(kept, STEPS + 1, 0, 1)

    load_force.wait()
    reorder(raw_force, source)

    load_volume.wait()
    load_lift.wait()
    row = lax.broadcasted_iota(jnp.int32, (64, 64), 0)
    column = lax.broadcasted_iota(jnp.int32, (64, 64), 1)
    weight = volume[...] - jnp.where(row == column, 0.1, 0.0).astype(F32)
    lifts = jnp.concatenate([lift[f] for f in range(6)], axis=0).T
    a_high, a_low = halves(jnp.concatenate([weight, lifts], axis=1))
    a_both = jnp.concatenate([a_high, a_low], axis=0)
    face_matrix = []
    for f in range(4):
        high, low = halves(lifts[:, 16 * f : 16 * f + 16])
        face_matrix.append(
            jnp.concatenate([high.astype(F32), high.astype(F32), low.astype(F32)], axis=1).astype(BF16)
        )

    @pl.when(jnp.logical_not(first))
    def _():
        for x in range(nx):
            start_copy(x).wait_recv()
        reorder(raw_start, fields.at[0])

    for step in range(STEPS):
        now = fields.at[step]
        last = step == STEPS - 1
        out = resid if last else fields.at[step + 1]
        if step > 0:
            send_faces(now, step, step, 0)

        def finish(cell, delta, now=now, out=out, last=last):
            value = now[cell] + delta + source[cell]
            out[cell] = value - kept[cell] if last else value

        inside(now, finish)
        outside(step, out, 1.0)

    def err_copy(x):
        part = pl.ds(x * ny, ny)
        return pltpu.make_async_remote_copy(
            src_ref=error.at[part], dst_ref=earlier.at[part],
            send_sem=err_send.at[x], recv_sem=err_recv.at[x],
            device_id={"tm": tm + 1, "sx": sx, "sy": sy}, device_id_type=MESH,
        )

    @pl.when(first)
    def _():
        for cell in range(cells):
            error[cell] = resid[cell]

    @pl.when(jnp.logical_not(first))
    def _():
        for x in range(nx):
            err_copy(x).wait_recv()

        def finish(cell, delta):
            error[cell] = resid[cell] + earlier[cell] + 4.0 * delta

        inside(earlier, finish)
        outside(STEPS, error, 4.0)

    @pl.when(more)
    def _():
        send_faces(error, STEPS, STEPS, 1)
        for x in range(nx):
            err_copy(x).start()

    @pl.when(first)
    def _():
        sent_faces(fields.at[0], 0, 0, 0)

    for step in range(1, STEPS):
        sent_faces(fields.at[step], step, step, 0)

    @pl.when(more)
    def _():
        sent_faces(kept, STEPS + 1, 0, 1)
        for x in range(nx):
            start_copy(x).wait_send()
            err_copy(x).wait_send()
        sent_faces(error, STEPS, STEPS, 1)


def finishing(nx, ny, kept, resid, error, corr_hbm, resid_hbm, out_c, out_r, out_sem):
    cells = nx * ny
    copies = []
    for part in range(4):
        low, rows = part * 16 * cells, 16 * cells
        for cell in range(cells):
            dofs = slice(part * 16, part * 16 + 16)
            value = resid[cell, dofs, :]
            out_r[pl.ds(low + cell, 16, stride=cells), :] = value
            out_c[pl.ds(low + cell, 16, stride=cells), :] = kept[cell, dofs, :] + error[cell, dofs, :]
        for i, (src, dst) in enumerate(((out_r, resid_hbm), (out_c, corr_hbm))):
            span = pl.ds(low, rows)
            copies.append(pltpu.make_async_copy(src.at[span], dst.at[span], out_sem.at[part, i]))
            copies[-1].start()
    for copy in copies:
        copy.wait()


def solution(mesh):
    counts = tuple(mesh.shape[axis] for axis in ("tm", "sx", "sy"))

    def local(slices_state, forcing, initial, volume, lift):
        _, dofs, nx, ny, nz = slices_state.shape
        cells = nx * ny
        rows = dofs * cells
        raw = pltpu.VMEM((rows, nz), F32)
        field = pltpu.VMEM((cells, dofs, nz), F32)
        stack = pltpu.VMEM((160, cells * nz), BF16)
        flat = jax.ShapeDtypeStruct((rows, nz), F32)
        shaped = jax.ShapeDtypeStruct((cells, dofs, nz), F32)
        vmem, hbm = pl.BlockSpec(memory_space=pltpu.VMEM), pl.BlockSpec(memory_space=pltpu.HBM)
        parts = pl.pallas_call(
            functools.partial(kernel, counts, nx, ny),
            out_shape=(shaped,) * 3,
            in_specs=[hbm] * 5,
            out_specs=(vmem,) * 3,
            scratch_shapes=[
                raw, raw, raw, pltpu.VMEM(volume.shape, F32), pltpu.VMEM((6, 16, dofs), F32),
                pltpu.VMEM((STEPS, cells, dofs, nz), F32), field, field,
                pltpu.VMEM((STEPS + 1, 2, ny, 16, nz), F32),
                pltpu.VMEM((STEPS + 1, 2, nx, 16, nz), F32),
                pltpu.VMEM((STEPS + 2, 2, nx, 16, nz), F32),
                stack, stack,
                pltpu.SemaphoreType.DMA((5,)),
                pltpu.SemaphoreType.DMA((STEPS + 2, 4)),
                pltpu.SemaphoreType.DMA((STEPS + 1, 4)),
                pltpu.SemaphoreType.DMA((nx,)),
                pltpu.SemaphoreType.DMA((nx,)),
                pltpu.SemaphoreType.DMA((nx,)),
                pltpu.SemaphoreType.DMA((nx,)),
            ],
            compiler_params=pltpu.CompilerParams(
                collective_id=0, has_side_effects=True, vmem_limit_bytes=32 * 2**20
            ),
            name="cycle",
        )(
            *(
                pltpu.with_memory_space_constraint(value, pltpu.HBM)
                for value in (
                    slices_state.reshape(rows, nz), forcing.reshape(rows, nz),
                    initial.reshape(rows, nz), volume, jnp.swapaxes(lift, 1, 2),
                )
            )
        )
        corrected, residual = pl.pallas_call(
            functools.partial(finishing, nx, ny),
            out_shape=(flat,) * 2,
            in_specs=[vmem] * 3,
            out_specs=(hbm,) * 2,
            scratch_shapes=[raw, raw, pltpu.SemaphoreType.DMA((4, 2))],
            compiler_params=pltpu.CompilerParams(vmem_limit_bytes=16 * 2**20),
            name="finishing",
        )(*parts)
        shape = slices_state.shape
        return corrected.reshape(shape), residual.reshape(shape)

    split = P("tm", None, "sx", "sy", None)
    return jax.shard_map(
        local,
        mesh=mesh,
        in_specs=(split, split, P(None, "sx", "sy", None), P(), P()),
        out_specs=(split, split),
        check_vma=False,
    )
```

```python
import functools

import jax
import jax.numpy as jnp
from jax import lax
from jax.experimental import pallas as pl
from jax.experimental.pallas import tpu as pltpu
from jax.sharding import PartitionSpec as P

MESH = pl.DeviceIdType.MESH
F32, BF16 = jnp.float32, jnp.bfloat16
STEPS = 4
WHOLE = (0, 2, 4)
PAIRED = (0, 2)
LANES = 128


def halves(value):
    high = value.astype(BF16)
    return high, (value - high.astype(F32)).astype(BF16)


def kernel(
    counts, nx, ny,
    state_hbm, force_hbm, init_hbm, vol_hbm, lift_hbm,
    kept, resid, error,
    raw_start, raw_state, raw_force, volume, lift,
    fields, source, earlier,
    halo_x, halo_y, sent_y, corner, edge, sent_edge, s_high, s_low,
    load_sem, face_send, face_recv, start_send, start_recv, err_send, err_recv,
    corner_send, corner_recv, edge_send, edge_recv,
):
    n_tm, n_sx, n_sy = counts
    cells = nx * ny
    tm, sx, sy = lax.axis_index("tm"), lax.axis_index("sx"), lax.axis_index("sy")
    first, more = tm == 0, tm < n_tm - 1
    exists = (sx < n_sx - 1, sx > 0, sy < n_sy - 1, sy > 0)
    comes = (sx > 0, sx < n_sx - 1, sy > 0, sy < n_sy - 1)
    shifts = ((1, 0), (-1, 0), (0, 1), (0, -1))
    diagonals = [(fx, fy) for fx in (0, 1) for fy in (2, 3)]

    def place(dt, f):
        dx, dy = shifts[f]
        return {"tm": tm + dt, "sx": sx + dx, "sy": sy + dy}

    def across(dt, fx, fy):
        return {"tm": tm + dt, "sx": sx + shifts[fx][0], "sy": sy + shifts[fy][1]}

    load_state = pltpu.make_async_copy(state_hbm, raw_state, load_sem.at[0])
    load_force = pltpu.make_async_copy(force_hbm, raw_force, load_sem.at[1])
    load_init = pltpu.make_async_copy(init_hbm, raw_start, load_sem.at[2])

    @pl.when(first)
    def _():
        load_init.start()

    load_state.start()
    load_force.start()
    load_volume = pltpu.make_async_copy(vol_hbm, volume, load_sem.at[3])
    load_lift = pltpu.make_async_copy(lift_hbm, lift, load_sem.at[4])
    load_volume.start()
    load_lift.start()

    barrier = pltpu.get_barrier_semaphore()

    def greet(dt, f):
        pl.semaphore_signal(barrier, inc=1, device_id=place(dt, f), device_id_type=MESH)

    for f in range(4):
        pl.when(exists[f])(functools.partial(greet, 0, f))
        pl.when(exists[f] & (tm > 0))(functools.partial(greet, -1, f))

    def greet_across(dt, fx, fy):
        pl.semaphore_signal(
            barrier, inc=1, device_id=across(dt, fx, fy), device_id_type=MESH
        )

    for fx, fy in diagonals:
        there = exists[fx] & exists[fy]
        pl.when(there)(functools.partial(greet_across, 0, fx, fy))
        pl.when(there & (tm > 0))(functools.partial(greet_across, -1, fx, fy))

    @pl.when(tm > 0)
    def _():
        pl.semaphore_signal(
            barrier, inc=1, device_id={"tm": tm - 1, "sx": sx, "sy": sy}, device_id_type=MESH
        )

    wide, tall = ny * LANES, cells * LANES
    for stack in (s_high, s_low):
        stack[64:80, 0:wide] = jnp.zeros((16, wide), BF16)
        stack[80:96, tall - wide : tall] = jnp.zeros((16, wide), BF16)
        for x in range(nx):
            low, high = x * wide, (x + 1) * wide
            stack[96:112, low : low + LANES] = jnp.zeros((16, LANES), BF16)
            stack[112:128, high - LANES : high] = jnp.zeros((16, LANES), BF16)

    def no_halo(f):
        ref = (halo_x, halo_x, halo_y, halo_y)[f]
        for phase in range(STEPS + 1):
            ref[phase, f % 2] = jnp.zeros(ref.shape[2:], F32)

    for f in range(4):
        pl.when(jnp.logical_not(comes[f]))(functools.partial(no_halo, f))

    def no_corner(fx, fy):
        for pair in range(STEPS // 2):
            corner[pair, fx, fy - 2] = jnp.zeros((16, LANES), F32)

    for fx, fy in diagonals:
        pl.when(jnp.logical_not(comes[fx] & comes[fy]))(functools.partial(no_corner, fx, fy))

    total = sum(e.astype(jnp.int32) for e in exists)
    total = total + sum((exists[fx] & exists[fy]).astype(jnp.int32) for fx, fy in diagonals)
    pl.semaphore_wait(barrier, total + jnp.where(more, total + 1, 0))

    def start_copy(x):
        part = pl.ds(x * 64 * ny, 64 * ny)
        return pltpu.make_async_remote_copy(
            src_ref=state_hbm.at[part], dst_ref=raw_start.at[part],
            send_sem=start_send.at[x], recv_sem=start_recv.at[x],
            device_id={"tm": tm + 1, "sx": sx, "sy": sy}, device_id_type=MESH,
        )

    @pl.when(more)
    def _():
        for x in range(nx):
            start_copy(x).start()

    top = lax.broadcasted_iota(jnp.int32, (8, LANES), 0) < 4
    lane = lax.broadcasted_iota(jnp.int32, (16, LANES), 1)

    def y_plus(ref, cell):
        parts = []
        for p in range(0, 64, 32):
            one, two = ref[cell, p + 8 : p + 16, :], ref[cell, p + 24 : p + 32, :]
            parts.append(jnp.where(top, pltpu.roll(one, 4, 0), two))
        return jnp.concatenate(parts, axis=0)

    def y_minus(ref, cell):
        parts = []
        for p in range(0, 64, 32):
            one, two = ref[cell, p : p + 8, :], ref[cell, p + 16 : p + 24, :]
            parts.append(jnp.where(top, one, pltpu.roll(two, 4, 0)))
        return jnp.concatenate(parts, axis=0)

    def face_copy(ref, slot, phase, dt, f, to=None):
        if f == 0:
            src = ref.at[pl.ds(cells - ny, ny), pl.ds(48, 16), :]
        elif f == 1:
            src = ref.at[pl.ds(0, ny), pl.ds(0, 16), :]
        else:
            src = sent_y.at[slot, f - 2]
        target = (halo_x, halo_x, halo_y, halo_y)[f].at[phase, f % 2]
        return pltpu.make_async_remote_copy(
            src_ref=src, dst_ref=target,
            send_sem=face_send.at[slot, f], recv_sem=face_recv.at[phase, f],
            device_id=place(dt, f if to is None else to), device_id_type=MESH,
        )

    def send_faces(ref, slot, phase, dt):
        if phase in WHOLE:
            odd = lax.rem(sx, 2) == 1
            pl.when(exists[0] & odd)(face_copy(ref, slot, phase, dt, 0).start)
            pl.when(exists[1])(face_copy(ref, slot, phase, dt, 1).start)
            pl.when(exists[0] & jnp.logical_not(odd))(face_copy(ref, slot, phase, dt, 0).start)
        for x in range(nx):
            sent_y[slot, 0, x] = y_plus(ref, x * ny + ny - 1)
            sent_y[slot, 1, x] = y_minus(ref, x * ny)
        for f in range(2, 4):
            pl.when(exists[f])(face_copy(ref, slot, phase, dt, f).start)
        if phase in PAIRED:
            for fx, fy in diagonals:
                pl.when(exists[fx] & exists[fy])(corner_copy(slot, phase, dt, fx, fy).start)

    def sent_faces(ref, slot, phase, dt):
        for f in range(4) if phase in WHOLE else range(2, 4):
            pl.when(exists[f])(face_copy(ref, slot, phase, dt, f).wait_send)
        if phase in PAIRED:
            for fx, fy in diagonals:
                pl.when(exists[fx] & exists[fy])(corner_copy(slot, phase, dt, fx, fy).wait_send)

    def corner_copy(slot, phase, dt, fx, fy, back=False):
        cell = nx - 1 if fx == 0 else 0
        pair = PAIRED.index(phase)
        target = across(dt, fx ^ 1, fy ^ 1) if back else across(dt, fx, fy)
        return pltpu.make_async_remote_copy(
            src_ref=sent_y.at[slot, fy - 2, cell], dst_ref=corner.at[pair, fx, fy - 2],
            send_sem=corner_send.at[slot, 2 * fx + fy - 2],
            recv_sem=corner_recv.at[pair, 2 * fx + fy - 2],
            device_id=target, device_id_type=MESH,
        )

    def edge_copy(pair, f, to=None):
        return pltpu.make_async_remote_copy(
            src_ref=sent_edge.at[pair, f], dst_ref=edge.at[pair, f],
            send_sem=edge_send.at[pair, f], recv_sem=edge_recv.at[pair, f],
            device_id=place(0, f if to is None else to), device_id_type=MESH,
        )

    def send_edges(pair, ref):
        for y in range(ny):
            sent_edge[pair, 0, y] = ref[cells - ny + y, 48:64, :]
            sent_edge[pair, 1, y] = ref[y, 0:16, :]
        for f in range(2):
            pl.when(exists[f])(edge_copy(pair, f).start)

    def next_faces(phase):
        pair, now = PAIRED.index(phase), fields.at[phase]
        for fx in range(2):

            @pl.when(comes[fx])
            def _(fx=fx):
                edge_copy(pair, fx, fx ^ 1).wait_recv()
                for fy in (2, 3):
                    back = corner_copy(0, phase, 0, fx, fy, True)
                    pl.when(comes[fy])(back.wait_recv)
                cell, low = (0, 0) if fx == 0 else (cells - ny, 48)
                own = [now[cell + y, low : low + 16, :] for y in range(ny)]
                none = [jnp.zeros((16, LANES), F32)] * (ny - 1)
                rows = []
                for blocks in (own, [corner[pair, fx, 0]] + none, none + [corner[pair, fx, 1]]):
                    high, part = halves(jnp.concatenate(blocks, axis=1))
                    rows += [high, part, high]
                added = jnp.dot(
                    edge_matrix[fx], jnp.concatenate(rows, axis=0), preferred_element_type=F32
                )
                for y in range(ny):
                    halo_x[phase + 1, fx, y] = edge[pair, fx, y] + added[:, y * LANES : (y + 1) * LANES]

    def reorder(raw, ref):
        for cell in range(cells):
            ref[cell] = raw[pl.ds(cell, 64, stride=cells), :]

    def inside(ref, finish, edges=None):
        def put(rows, cell, value):
            high, low = halves(value)
            cols = slice(cell * LANES, (cell + 1) * LANES)
            s_high[rows : rows + value.shape[0], cols] = high
            s_low[rows : rows + value.shape[0], cols] = low

        for x in range(nx):
            for y in range(ny):
                cell = x * ny + y
                pair = halves(ref[cell])
                for stack, half in zip((s_high, s_low), pair):
                    stack[0:64, cell * LANES : (cell + 1) * LANES] = half
                    if x + 1 < nx:
                        stack[64:80, (cell + ny) * LANES : (cell + ny + 1) * LANES] = half[48:64]
                    if x > 0:
                        stack[80:96, (cell - ny) * LANES : (cell - ny + 1) * LANES] = half[0:16]
                if y + 1 < ny:
                    put(96, cell + 1, y_plus(ref, cell))
                if y > 0:
                    put(112, cell - 1, y_minus(ref, cell))
                up = pltpu.roll(ref[cell, pl.ds(3, 16, stride=4), :], 1, 1)
                put(128, cell, jnp.where(lane == 0, 0.0, up))
                down = pltpu.roll(ref[cell, pl.ds(0, 16, stride=4), :], LANES - 1, 1)
                put(144, cell, jnp.where(lane == LANES - 1, 0.0, down))
        order = list(dict.fromkeys([0, nx - 1] + list(range(nx))))
        for turn, x in enumerate(order):
            if edges is not None and turn == min(2, nx):
                edges()
            cols = slice(x * wide, (x + 1) * wide)
            both = jnp.dot(a_both, s_high[:, cols], preferred_element_type=F32)
            rest = jnp.dot(a_high, s_low[:, cols], preferred_element_type=F32)
            delta = both[:64] + both[64:] + rest
            for y in range(ny):
                finish(x * ny + y, delta[:, y * LANES : (y + 1) * LANES])

    def outside(phase, out, scale):
        for faces in ((2, 3), (0, 1)):
            for f in faces:
                if f < 2 and phase not in WHOLE:
                    continue
                pl.when(comes[f])(face_copy(kept, STEPS + 1, phase, 0, f, f ^ 1).wait_recv)
            for f in faces:
                ref = (halo_x, halo_x, halo_y, halo_y)[f]
                count = ref.shape[2]
                trace = jnp.concatenate([ref[phase, f % 2, i] for i in range(count)], axis=1)
                high, low = halves(trace)
                added = jnp.dot(
                    face_matrix[f], jnp.concatenate([high, low, high], axis=0), preferred_element_type=F32
                )
                if scale != 1.0:
                    added = scale * added
                for i in range(count):
                    cell = (i, cells - ny + i, i * ny, i * ny + ny - 1)[f]
                    out[cell] = out[cell] + added[:, i * LANES : (i + 1) * LANES]

    @pl.when(first)
    def _():
        load_init.wait()
        reorder(raw_start, fields.at[0])
        send_faces(fields.at[0], 0, 0, 0)

    load_state.wait()
    reorder(raw_state, kept)

    @pl.when(more)
    def _():
        send_faces(kept, STEPS + 1, 0, 1)

    load_force.wait()
    reorder(raw_force, source)

    load_volume.wait()
    load_lift.wait()
    row = lax.broadcasted_iota(jnp.int32, (64, 64), 0)
    column = lax.broadcasted_iota(jnp.int32, (64, 64), 1)
    weight = volume[...] - jnp.where(row == column, 0.1, 0.0).astype(F32)
    lifts = jnp.concatenate([lift[f] for f in range(6)], axis=0).T
    a_high, a_low = halves(jnp.concatenate([weight, lifts], axis=1))
    a_both = jnp.concatenate([a_high, a_low], axis=0)
    thirds = []
    for f in range(4):
        high, low = halves(lifts[:, 16 * f : 16 * f + 16])
        thirds.append(jnp.concatenate([high.astype(F32), high.astype(F32), low.astype(F32)], axis=1))
    face_matrix = [third.astype(BF16) for third in thirds]
    edge_matrix = []
    for fx, low in ((0, 48), (1, 0)):
        rows = [thirds[f][low : low + 16] for f in (1 - fx, 2, 3)]
        edge_matrix.append(jnp.concatenate(rows, axis=1).astype(BF16))

    @pl.when(jnp.logical_not(first))
    def _():
        for x in range(nx):
            start_copy(x).wait_recv()
        reorder(raw_start, fields.at[0])

    for step in range(STEPS):
        now = fields.at[step]
        last = step == STEPS - 1
        out = resid if last else fields.at[step + 1]
        if step > 0:
            send_faces(now, step, step, 0)

        def finish(cell, delta, now=now, out=out, last=last):
            value = now[cell] + delta + source[cell]
            out[cell] = value - kept[cell] if last else value

        if step in PAIRED:
            inside(now, finish, functools.partial(send_edges, PAIRED.index(step), out))
        else:
            inside(now, finish)
            next_faces(step - 1)
        outside(step, out, 1.0)

    def err_copy(x):
        part = pl.ds(x * ny, ny)
        return pltpu.make_async_remote_copy(
            src_ref=error.at[part], dst_ref=earlier.at[part],
            send_sem=err_send.at[x], recv_sem=err_recv.at[x],
            device_id={"tm": tm + 1, "sx": sx, "sy": sy}, device_id_type=MESH,
        )

    @pl.when(first)
    def _():
        for cell in range(cells):
            error[cell] = resid[cell]

    @pl.when(jnp.logical_not(first))
    def _():
        for x in range(nx):
            err_copy(x).wait_recv()

        def finish(cell, delta):
            error[cell] = resid[cell] + earlier[cell] + 4.0 * delta

        inside(earlier, finish)
        outside(STEPS, error, 4.0)

    @pl.when(more)
    def _():
        send_faces(error, STEPS, STEPS, 1)
        for x in range(nx):
            err_copy(x).start()

    @pl.when(first)
    def _():
        sent_faces(fields.at[0], 0, 0, 0)

    for step in range(1, STEPS):
        sent_faces(fields.at[step], step, step, 0)
    for pair in range(len(PAIRED)):
        for f in range(2):
            pl.when(exists[f])(edge_copy(pair, f).wait_send)

    @pl.when(more)
    def _():
        sent_faces(kept, STEPS + 1, 0, 1)
        for x in range(nx):
            start_copy(x).wait_send()
            err_copy(x).wait_send()
        sent_faces(error, STEPS, STEPS, 1)


def finishing(nx, ny, kept, resid, error, corr_hbm, resid_hbm, out_c, out_r, out_sem):
    cells = nx * ny
    copies = []
    for part in range(4):
        low, rows = part * 16 * cells, 16 * cells
        for cell in range(cells):
            dofs = slice(part * 16, part * 16 + 16)
            value = resid[cell, dofs, :]
            out_r[pl.ds(low + cell, 16, stride=cells), :] = value
            out_c[pl.ds(low + cell, 16, stride=cells), :] = kept[cell, dofs, :] + error[cell, dofs, :]
        for i, (src, dst) in enumerate(((out_r, resid_hbm), (out_c, corr_hbm))):
            span = pl.ds(low, rows)
            copies.append(pltpu.make_async_copy(src.at[span], dst.at[span], out_sem.at[part, i]))
            copies[-1].start()
    for copy in copies:
        copy.wait()


def solution(mesh):
    counts = tuple(mesh.shape[axis] for axis in ("tm", "sx", "sy"))

    def local(slices_state, forcing, initial, volume, lift):
        _, dofs, nx, ny, nz = slices_state.shape
        cells = nx * ny
        rows = dofs * cells
        raw = pltpu.VMEM((rows, nz), F32)
        field = pltpu.VMEM((cells, dofs, nz), F32)
        stack = pltpu.VMEM((160, cells * nz), BF16)
        flat = jax.ShapeDtypeStruct((rows, nz), F32)
        shaped = jax.ShapeDtypeStruct((cells, dofs, nz), F32)
        vmem, hbm = pl.BlockSpec(memory_space=pltpu.VMEM), pl.BlockSpec(memory_space=pltpu.HBM)
        parts = pl.pallas_call(
            functools.partial(kernel, counts, nx, ny),
            out_shape=(shaped,) * 3,
            in_specs=[hbm] * 5,
            out_specs=(vmem,) * 3,
            scratch_shapes=[
                raw, raw, raw, pltpu.VMEM(volume.shape, F32), pltpu.VMEM((6, 16, dofs), F32),
                pltpu.VMEM((STEPS, cells, dofs, nz), F32), field, field,
                pltpu.VMEM((STEPS + 1, 2, ny, 16, nz), F32),
                pltpu.VMEM((STEPS + 1, 2, nx, 16, nz), F32),
                pltpu.VMEM((STEPS + 2, 2, nx, 16, nz), F32),
                pltpu.VMEM((STEPS // 2, 2, 2, 16, nz), F32),
                pltpu.VMEM((STEPS // 2, 2, ny, 16, nz), F32),
                pltpu.VMEM((STEPS // 2, 2, ny, 16, nz), F32),
                stack, stack,
                pltpu.SemaphoreType.DMA((5,)),
                pltpu.SemaphoreType.DMA((STEPS + 2, 4)),
                pltpu.SemaphoreType.DMA((STEPS + 1, 4)),
                pltpu.SemaphoreType.DMA((nx,)),
                pltpu.SemaphoreType.DMA((nx,)),
                pltpu.SemaphoreType.DMA((nx,)),
                pltpu.SemaphoreType.DMA((nx,)),
                pltpu.SemaphoreType.DMA((STEPS + 2, 4)),
                pltpu.SemaphoreType.DMA((STEPS // 2, 4)),
                pltpu.SemaphoreType.DMA((STEPS // 2, 2)),
                pltpu.SemaphoreType.DMA((STEPS // 2, 2)),
            ],
            compiler_params=pltpu.CompilerParams(
                collective_id=0, has_side_effects=True, vmem_limit_bytes=32 * 2**20
            ),
            name="cycle",
        )(
            *(
                pltpu.with_memory_space_constraint(value, pltpu.HBM)
                for value in (
                    slices_state.reshape(rows, nz), forcing.reshape(rows, nz),
                    initial.reshape(rows, nz), volume, jnp.swapaxes(lift, 1, 2),
                )
            )
        )
        corrected, residual = pl.pallas_call(
            functools.partial(finishing, nx, ny),
            out_shape=(flat,) * 2,
            in_specs=[vmem] * 3,
            out_specs=(hbm,) * 2,
            scratch_shapes=[raw, raw, pltpu.SemaphoreType.DMA((4, 2))],
            compiler_params=pltpu.CompilerParams(vmem_limit_bytes=16 * 2**20),
            name="finishing",
        )(*parts)
        shape = slices_state.shape
        return corrected.reshape(shape), residual.reshape(shape)

    split = P("tm", None, "sx", "sy", None)
    return jax.shard_map(
        local,
        mesh=mesh,
        in_specs=(split, split, P(None, "sx", "sy", None), P(), P()),
        out_specs=(split, split),
        check_vma=False,
    )
```

```python
import functools

import jax
import jax.numpy as jnp
from jax import lax
from jax.experimental import pallas as pl
from jax.experimental.pallas import tpu as pltpu
from jax.sharding import PartitionSpec as P

MESH = pl.DeviceIdType.MESH
F32, BF16 = jnp.float32, jnp.bfloat16
STEPS = 4
LANES = 128


def halves(value):
    high = value.astype(BF16)
    return high, (value - high.astype(F32)).astype(BF16)


def kernel(
    counts, nx, ny,
    state_hbm, force_hbm, init_hbm, vol_hbm, lift_hbm,
    kept, resid, error,
    raw_start, raw_state, raw_force, volume, lift,
    fields, added,
    halo_x, halo_y, sent_y, s_high, s_low,
    load_sem, face_send, face_recv, start_send, start_recv, err_send, err_recv,
):
    n_tm, n_sx, n_sy = counts
    cells = nx * ny
    tm, sx, sy = lax.axis_index("tm"), lax.axis_index("sx"), lax.axis_index("sy")
    first, more = tm == 0, tm < n_tm - 1
    exists = (sx < n_sx - 1, sx > 0, sy < n_sy - 1, sy > 0)
    comes = (sx > 0, sx < n_sx - 1, sy > 0, sy < n_sy - 1)
    shifts = ((1, 0), (-1, 0), (0, 1), (0, -1))

    def place(dt, f):
        dx, dy = shifts[f]
        return {"tm": tm + dt, "sx": sx + dx, "sy": sy + dy}

    load_state = pltpu.make_async_copy(state_hbm, raw_state, load_sem.at[0])
    load_force = pltpu.make_async_copy(force_hbm, raw_force, load_sem.at[1])
    load_init = pltpu.make_async_copy(init_hbm, raw_start, load_sem.at[2])

    @pl.when(first)
    def _():
        load_init.start()

    load_state.start()
    load_force.start()
    load_volume = pltpu.make_async_copy(vol_hbm, volume, load_sem.at[3])
    load_lift = pltpu.make_async_copy(lift_hbm, lift, load_sem.at[4])
    load_volume.start()
    load_lift.start()

    barrier = pltpu.get_barrier_semaphore()

    def greet(dt, f):
        pl.semaphore_signal(barrier, inc=1, device_id=place(dt, f), device_id_type=MESH)

    for f in range(4):
        pl.when(exists[f])(functools.partial(greet, 0, f))
        pl.when(exists[f] & (tm > 0))(functools.partial(greet, -1, f))

    @pl.when(tm > 0)
    def _():
        pl.semaphore_signal(
            barrier, inc=1, device_id={"tm": tm - 1, "sx": sx, "sy": sy}, device_id_type=MESH
        )

    wide, tall = ny * LANES, cells * LANES
    for stack in (s_high, s_low):
        stack[64:80, 0:wide] = jnp.zeros((16, wide), BF16)
        stack[80:96, tall - wide : tall] = jnp.zeros((16, wide), BF16)
        for x in range(nx):
            low, high = x * wide, (x + 1) * wide
            stack[96:112, low : low + LANES] = jnp.zeros((16, LANES), BF16)
            stack[112:128, high - LANES : high] = jnp.zeros((16, LANES), BF16)

    def no_halo(f):
        ref = (halo_x, halo_x, halo_y, halo_y)[f]
        for phase in range(STEPS + 1):
            ref[phase, f % 2] = jnp.zeros(ref.shape[2:], F32)

    for f in range(4):
        pl.when(jnp.logical_not(comes[f]))(functools.partial(no_halo, f))

    total = sum(e.astype(jnp.int32) for e in exists)
    pl.semaphore_wait(barrier, total + jnp.where(more, total + 1, 0))

    def start_copy(x):
        part = pl.ds(x * 64 * ny, 64 * ny)
        return pltpu.make_async_remote_copy(
            src_ref=state_hbm.at[part], dst_ref=raw_start.at[part],
            send_sem=start_send.at[x], recv_sem=start_recv.at[x],
            device_id={"tm": tm + 1, "sx": sx, "sy": sy}, device_id_type=MESH,
        )

    @pl.when(more)
    def _():
        for x in range(nx):
            start_copy(x).start()

    top = lax.broadcasted_iota(jnp.int32, (8, LANES), 0) < 4
    lane = lax.broadcasted_iota(jnp.int32, (16, LANES), 1)

    def y_plus(ref, cell):
        parts = []
        for p in range(0, 64, 32):
            one, two = ref[cell, p + 8 : p + 16, :], ref[cell, p + 24 : p + 32, :]
            parts.append(jnp.where(top, pltpu.roll(one, 4, 0), two))
        return jnp.concatenate(parts, axis=0)

    def y_minus(ref, cell):
        parts = []
        for p in range(0, 64, 32):
            one, two = ref[cell, p : p + 8, :], ref[cell, p + 16 : p + 24, :]
            parts.append(jnp.where(top, one, pltpu.roll(two, 4, 0)))
        return jnp.concatenate(parts, axis=0)

    def face_copy(ref, slot, phase, dt, f, to=None):
        if f == 0:
            src = ref.at[pl.ds(cells - ny, ny), pl.ds(48, 16), :]
        elif f == 1:
            src = ref.at[pl.ds(0, ny), pl.ds(0, 16), :]
        else:
            src = sent_y.at[slot, f - 2]
        target = (halo_x, halo_x, halo_y, halo_y)[f].at[phase, f % 2]
        return pltpu.make_async_remote_copy(
            src_ref=src, dst_ref=target,
            send_sem=face_send.at[slot, f], recv_sem=face_recv.at[phase, f],
            device_id=place(dt, f if to is None else to), device_id_type=MESH,
        )

    def send_faces(ref, slot, phase, dt):
        odd = lax.rem(sx, 2) == 1
        pl.when(exists[0] & odd)(face_copy(ref, slot, phase, dt, 0).start)
        pl.when(exists[1])(face_copy(ref, slot, phase, dt, 1).start)
        pl.when(exists[0] & jnp.logical_not(odd))(face_copy(ref, slot, phase, dt, 0).start)
        for x in range(nx):
            sent_y[slot, 0, x] = y_plus(ref, x * ny + ny - 1)
            sent_y[slot, 1, x] = y_minus(ref, x * ny)
        for f in range(2, 4):
            pl.when(exists[f])(face_copy(ref, slot, phase, dt, f).start)

    def sent_faces(ref, slot, phase, dt):
        for f in range(4):
            pl.when(exists[f])(face_copy(ref, slot, phase, dt, f).wait_send)

    def reorder(raw, ref):
        for cell in range(cells):
            ref[cell] = raw[pl.ds(cell, 64, stride=cells), :]

    def inside(ref, finish):
        def put(rows, cell, value):
            high, low = halves(value)
            cols = slice(cell * LANES, (cell + 1) * LANES)
            s_high[rows : rows + value.shape[0], cols] = high
            s_low[rows : rows + value.shape[0], cols] = low

        for x in range(nx):
            for y in range(ny):
                cell = x * ny + y
                pair = halves(ref[cell])
                for stack, half in zip((s_high, s_low), pair):
                    stack[0:64, cell * LANES : (cell + 1) * LANES] = half
                    if x + 1 < nx:
                        stack[64:80, (cell + ny) * LANES : (cell + ny + 1) * LANES] = half[48:64]
                    if x > 0:
                        stack[80:96, (cell - ny) * LANES : (cell - ny + 1) * LANES] = half[0:16]
                if y + 1 < ny:
                    put(96, cell + 1, y_plus(ref, cell))
                if y > 0:
                    put(112, cell - 1, y_minus(ref, cell))
                up = pltpu.roll(ref[cell, pl.ds(3, 16, stride=4), :], 1, 1)
                put(128, cell, jnp.where(lane == 0, 0.0, up))
                down = pltpu.roll(ref[cell, pl.ds(0, 16, stride=4), :], LANES - 1, 1)
                put(144, cell, jnp.where(lane == LANES - 1, 0.0, down))
        for x in range(nx):
            cols = slice(x * wide, (x + 1) * wide)
            both = jnp.dot(a_both, s_high[:, cols], preferred_element_type=F32)
            rest = jnp.dot(a_high, s_low[:, cols], preferred_element_type=F32)
            delta = both[:64] + both[64:] + rest
            for y in range(ny):
                finish(x * ny + y, delta[:, y * LANES : (y + 1) * LANES])

    def outside(phase, out, scale):
        for faces in ((2, 3), (0, 1)):
            for f in faces:
                pl.when(comes[f])(face_copy(kept, STEPS + 1, phase, 0, f, f ^ 1).wait_recv)
            for f in faces:
                ref = (halo_x, halo_x, halo_y, halo_y)[f]
                count = ref.shape[2]
                trace = jnp.concatenate([ref[phase, f % 2, i] for i in range(count)], axis=1)
                high, low = halves(trace)
                more_delta = scale * jnp.dot(
                    face_matrix[f], jnp.concatenate([high, low, high], axis=0), preferred_element_type=F32
                )
                for i in range(count):
                    cell = (i, cells - ny + i, i * ny, i * ny + ny - 1)[f]
                    out[cell] = out[cell] + more_delta[:, i * LANES : (i + 1) * LANES]

    @pl.when(first)
    def _():
        load_init.wait()
        reorder(raw_start, fields.at[0])

    load_state.wait()
    reorder(raw_state, kept)

    @pl.when(more)
    def _():
        send_faces(kept, STEPS + 1, 0, 1)

    load_force.wait()
    reorder(raw_force, added.at[0])

    load_volume.wait()
    load_lift.wait()
    row = lax.broadcasted_iota(jnp.int32, (64, 64), 0)
    column = lax.broadcasted_iota(jnp.int32, (64, 64), 1)
    weight = volume[...] - jnp.where(row == column, 0.1, 0.0).astype(F32)
    lifts = jnp.concatenate([lift[f] for f in range(6)], axis=0).T
    a_high, a_low = halves(jnp.concatenate([weight, lifts], axis=1))
    a_both = jnp.concatenate([a_high, a_low], axis=0)
    face_matrix = []
    for f in range(4):
        high, low = halves(lifts[:, 16 * f : 16 * f + 16])
        face_matrix.append(
            jnp.concatenate([high.astype(F32), high.astype(F32), low.astype(F32)], axis=1).astype(BF16)
        )

    @pl.when(jnp.logical_not(first))
    def _():
        for x in range(nx):
            start_copy(x).wait_recv()
        reorder(raw_start, fields.at[0])

    def err_copy(x):
        part = pl.ds(x * ny, ny)
        return pltpu.make_async_remote_copy(
            src_ref=fields.at[STEPS + 2, part], dst_ref=fields.at[STEPS + 1, part],
            send_sem=err_send.at[x], recv_sem=err_recv.at[x],
            device_id={"tm": tm + 1, "sx": sx, "sy": sy}, device_id_type=MESH,
        )

    def advance(turn, _):
        coarse = turn == STEPS
        place_in = turn + coarse.astype(jnp.int32)
        now, out = fields.at[place_in], fields.at[place_in + 1]
        adding = added.at[coarse.astype(jnp.int32)]
        scale = jnp.where(coarse, 4.0, 1.0).astype(F32)

        @pl.when(((turn > 0) | first) & (turn < STEPS))
        def _():
            send_faces(now, turn, turn, 0)

        @pl.when(coarse)
        def _():
            for x in range(nx):
                err_copy(x).wait_recv()

        def finish(cell, delta):
            out[cell] = now[cell] + scale * delta + adding[cell]

        inside(now, finish)
        outside(turn, out, scale)

        @pl.when(turn == STEPS - 1)
        def _():
            for cell in range(cells):
                value = fields[STEPS, cell] - kept[cell]
                resid[cell] = value
                added[1, cell] = value
                fields[STEPS + 2, cell] = value

        return 0

    lax.fori_loop(0, jnp.where(first, STEPS, STEPS + 1), advance, 0)

    @pl.when(more)
    def _():
        send_faces(fields.at[STEPS + 2], STEPS, STEPS, 1)
        for x in range(nx):
            err_copy(x).start()

    for cell in range(cells):
        error[cell] = fields[STEPS + 2, cell]

    @pl.when(first)
    def _():
        sent_faces(fields.at[0], 0, 0, 0)

    def sent_turn(turn, _):
        sent_faces(fields.at[turn], turn, turn, 0)
        return 0

    lax.fori_loop(1, STEPS, sent_turn, 0)

    @pl.when(more)
    def _():
        sent_faces(kept, STEPS + 1, 0, 1)
        for x in range(nx):
            start_copy(x).wait_send()
            err_copy(x).wait_send()
        sent_faces(fields.at[STEPS + 2], STEPS, STEPS, 1)


def finishing(nx, ny, kept, resid, error, corr_hbm, resid_hbm, out_c, out_r, out_sem):
    cells = nx * ny
    copies = []
    for part in range(4):
        low, rows = part * 16 * cells, 16 * cells
        for cell in range(cells):
            dofs = slice(part * 16, part * 16 + 16)
            value = resid[cell, dofs, :]
            out_r[pl.ds(low + cell, 16, stride=cells), :] = value
            out_c[pl.ds(low + cell, 16, stride=cells), :] = kept[cell, dofs, :] + error[cell, dofs, :]
        for i, (src, dst) in enumerate(((out_r, resid_hbm), (out_c, corr_hbm))):
            span = pl.ds(low, rows)
            copies.append(pltpu.make_async_copy(src.at[span], dst.at[span], out_sem.at[part, i]))
            copies[-1].start()
    for copy in copies:
        copy.wait()


def solution(mesh):
    counts = tuple(mesh.shape[axis] for axis in ("tm", "sx", "sy"))

    def local(slices_state, forcing, initial, volume, lift):
        _, dofs, nx, ny, nz = slices_state.shape
        cells = nx * ny
        rows = dofs * cells
        raw = pltpu.VMEM((rows, nz), F32)
        stack = pltpu.VMEM((160, cells * nz), BF16)
        flat = jax.ShapeDtypeStruct((rows, nz), F32)
        shaped = jax.ShapeDtypeStruct((cells, dofs, nz), F32)
        vmem, hbm = pl.BlockSpec(memory_space=pltpu.VMEM), pl.BlockSpec(memory_space=pltpu.HBM)
        parts = pl.pallas_call(
            functools.partial(kernel, counts, nx, ny),
            out_shape=(shaped,) * 3,
            in_specs=[hbm] * 5,
            out_specs=(vmem,) * 3,
            scratch_shapes=[
                raw, raw, raw, pltpu.VMEM(volume.shape, F32), pltpu.VMEM((6, 16, dofs), F32),
                pltpu.VMEM((STEPS + 3, cells, dofs, nz), F32), pltpu.VMEM((2, cells, dofs, nz), F32),
                pltpu.VMEM((STEPS + 1, 2, ny, 16, nz), F32),
                pltpu.VMEM((STEPS + 1, 2, nx, 16, nz), F32),
                pltpu.VMEM((STEPS + 2, 2, nx, 16, nz), F32),
                stack, stack,
                pltpu.SemaphoreType.DMA((5,)),
                pltpu.SemaphoreType.DMA((STEPS + 2, 4)),
                pltpu.SemaphoreType.DMA((STEPS + 1, 4)),
                pltpu.SemaphoreType.DMA((nx,)),
                pltpu.SemaphoreType.DMA((nx,)),
                pltpu.SemaphoreType.DMA((nx,)),
                pltpu.SemaphoreType.DMA((nx,)),
            ],
            compiler_params=pltpu.CompilerParams(
                collective_id=0, has_side_effects=True, vmem_limit_bytes=32 * 2**20
            ),
            name="cycle",
        )(
            *(
                pltpu.with_memory_space_constraint(value, pltpu.HBM)
                for value in (
                    slices_state.reshape(rows, nz), forcing.reshape(rows, nz),
                    initial.reshape(rows, nz), volume, jnp.swapaxes(lift, 1, 2),
                )
            )
        )
        corrected, residual = pl.pallas_call(
            functools.partial(finishing, nx, ny),
            out_shape=(flat,) * 2,
            in_specs=[vmem] * 3,
            out_specs=(hbm,) * 2,
            scratch_shapes=[raw, raw, pltpu.SemaphoreType.DMA((4, 2))],
            compiler_params=pltpu.CompilerParams(vmem_limit_bytes=16 * 2**20),
            name="finishing",
        )(*parts)
        shape = slices_state.shape
        return corrected.reshape(shape), residual.reshape(shape)

    split = P("tm", None, "sx", "sy", None)
    return jax.shard_map(
        local,
        mesh=mesh,
        in_specs=(split, split, P(None, "sx", "sy", None), P(), P()),
        out_specs=(split, split),
        check_vma=False,
    )
```

```python
import functools

import jax
import jax.numpy as jnp
from jax import lax
from jax.experimental import pallas as pl
from jax.experimental.pallas import tpu as pltpu
from jax.sharding import PartitionSpec as P

MESH = pl.DeviceIdType.MESH
F32, BF16 = jnp.float32, jnp.bfloat16
STEPS = 4
LANES = 128


def halves(value):
    high = value.astype(BF16)
    return high, (value - high.astype(F32)).astype(BF16)


def kernel(
    counts, nx, ny,
    state_hbm, force_hbm, init_hbm, vol_hbm, lift_hbm,
    kept, resid, error,
    raw_start, raw_state, raw_force, volume, lift,
    fields, source, earlier,
    halo_x, halo_y, sent_y, stack, lows,
    load_sem, face_send, face_recv, start_send, start_recv, err_send, err_recv,
):
    n_tm, n_sx, n_sy = counts
    cells = nx * ny
    tm, sx, sy = lax.axis_index("tm"), lax.axis_index("sx"), lax.axis_index("sy")
    first, more = tm == 0, tm < n_tm - 1
    exists = (sx < n_sx - 1, sx > 0, sy < n_sy - 1, sy > 0)
    comes = (sx > 0, sx < n_sx - 1, sy > 0, sy < n_sy - 1)
    shifts = ((1, 0), (-1, 0), (0, 1), (0, -1))

    def place(dt, f):
        dx, dy = shifts[f]
        return {"tm": tm + dt, "sx": sx + dx, "sy": sy + dy}

    load_state = pltpu.make_async_copy(state_hbm, raw_state, load_sem.at[0])
    load_force = pltpu.make_async_copy(force_hbm, raw_force, load_sem.at[1])
    load_init = pltpu.make_async_copy(init_hbm, raw_start, load_sem.at[2])

    @pl.when(first)
    def _():
        load_init.start()

    load_state.start()
    load_force.start()
    load_volume = pltpu.make_async_copy(vol_hbm, volume, load_sem.at[3])
    load_lift = pltpu.make_async_copy(lift_hbm, lift, load_sem.at[4])
    load_volume.start()
    load_lift.start()

    barrier = pltpu.get_barrier_semaphore()

    def greet(dt, f):
        pl.semaphore_signal(barrier, inc=1, device_id=place(dt, f), device_id_type=MESH)

    for f in range(4):
        pl.when(exists[f])(functools.partial(greet, 0, f))
        pl.when(exists[f] & (tm > 0))(functools.partial(greet, -1, f))

    @pl.when(tm > 0)
    def _():
        pl.semaphore_signal(
            barrier, inc=1, device_id={"tm": tm - 1, "sx": sx, "sy": sy}, device_id_type=MESH
        )

    wide, tall = ny * LANES, cells * LANES
    for shift in (0, 96):
        stack[64 + shift : 80 + shift, 0:wide] = jnp.zeros((16, wide), BF16)
        stack[80 + shift : 96 + shift, tall - wide : tall] = jnp.zeros((16, wide), BF16)
        for x in range(nx):
            left, right = x * wide, (x + 1) * wide
            stack[96 + shift : 112 + shift, left : left + LANES] = jnp.zeros((16, LANES), BF16)
            stack[112 + shift : 128 + shift, right - LANES : right] = jnp.zeros((16, LANES), BF16)

    def no_halo(f):
        ref = (halo_x, halo_x, halo_y, halo_y)[f]
        for phase in range(STEPS + 1):
            ref[phase, f % 2] = jnp.zeros(ref.shape[2:], F32)

    for f in range(4):
        pl.when(jnp.logical_not(comes[f]))(functools.partial(no_halo, f))

    total = sum(e.astype(jnp.int32) for e in exists)
    pl.semaphore_wait(barrier, total + jnp.where(more, total + 1, 0))

    def start_copy(x):
        part = pl.ds(x * 64 * ny, 64 * ny)
        return pltpu.make_async_remote_copy(
            src_ref=state_hbm.at[part], dst_ref=raw_start.at[part],
            send_sem=start_send.at[x], recv_sem=start_recv.at[x],
            device_id={"tm": tm + 1, "sx": sx, "sy": sy}, device_id_type=MESH,
        )

    @pl.when(more)
    def _():
        for x in range(nx):
            start_copy(x).start()

    top = lax.broadcasted_iota(jnp.int32, (8, LANES), 0) < 4
    lane = lax.broadcasted_iota(jnp.int32, (16, LANES), 1)

    def y_plus(ref, cell):
        parts = []
        for p in range(0, 64, 32):
            one, two = ref[cell, p + 8 : p + 16, :], ref[cell, p + 24 : p + 32, :]
            parts.append(jnp.where(top, pltpu.roll(one, 4, 0), two))
        return jnp.concatenate(parts, axis=0)

    def y_minus(ref, cell):
        parts = []
        for p in range(0, 64, 32):
            one, two = ref[cell, p : p + 8, :], ref[cell, p + 16 : p + 24, :]
            parts.append(jnp.where(top, one, pltpu.roll(two, 4, 0)))
        return jnp.concatenate(parts, axis=0)

    def face_copy(ref, slot, phase, dt, f, to=None):
        if f == 0:
            src = ref.at[pl.ds(cells - ny, ny), pl.ds(48, 16), :]
        elif f == 1:
            src = ref.at[pl.ds(0, ny), pl.ds(0, 16), :]
        else:
            src = sent_y.at[slot, f - 2]
        target = (halo_x, halo_x, halo_y, halo_y)[f].at[phase, f % 2]
        return pltpu.make_async_remote_copy(
            src_ref=src, dst_ref=target,
            send_sem=face_send.at[slot, f], recv_sem=face_recv.at[phase, f],
            device_id=place(dt, f if to is None else to), device_id_type=MESH,
        )

    def send_faces(ref, slot, phase, dt):
        odd = lax.rem(sx, 2) == 1
        pl.when(exists[0] & odd)(face_copy(ref, slot, phase, dt, 0).start)
        pl.when(exists[1])(face_copy(ref, slot, phase, dt, 1).start)
        pl.when(exists[0] & jnp.logical_not(odd))(face_copy(ref, slot, phase, dt, 0).start)
        for x in range(nx):
            sent_y[slot, 0, x] = y_plus(ref, x * ny + ny - 1)
            sent_y[slot, 1, x] = y_minus(ref, x * ny)
        for f in range(2, 4):
            pl.when(exists[f])(face_copy(ref, slot, phase, dt, f).start)

    def sent_faces(ref, slot, phase, dt):
        for f in range(4):
            pl.when(exists[f])(face_copy(ref, slot, phase, dt, f).wait_send)

    def reorder(raw, ref):
        for cell in range(cells):
            ref[cell] = raw[pl.ds(cell, 64, stride=cells), :]

    def inside(ref, finish):
        def put(rows, cell, pair):
            cols = slice(cell * LANES, (cell + 1) * LANES)
            stack[rows : rows + 16, cols] = pair[0]
            stack[rows + 96 : rows + 112, cols] = pair[1]

        for x in range(nx):
            for y in range(ny):
                cell = x * ny + y
                high, low = halves(ref[cell])
                stack[0:64, cell * LANES : (cell + 1) * LANES] = high
                lows[x * 64 : (x + 1) * 64, y * LANES : (y + 1) * LANES] = low
                if x + 1 < nx:
                    put(64, cell + ny, (high[48:64], low[48:64]))
                if x > 0:
                    put(80, cell - ny, (high[0:16], low[0:16]))
                if y + 1 < ny:
                    put(96, cell + 1, halves(y_plus(ref, cell)))
                if y > 0:
                    put(112, cell - 1, halves(y_minus(ref, cell)))
                up = pltpu.roll(ref[cell, pl.ds(3, 16, stride=4), :], 1, 1)
                put(128, cell, halves(jnp.where(lane == 0, 0.0, up)))
                down = pltpu.roll(ref[cell, pl.ds(0, 16, stride=4), :], LANES - 1, 1)
                put(144, cell, halves(jnp.where(lane == LANES - 1, 0.0, down)))
        rest = jnp.dot(low_matrix, lows[...], preferred_element_type=F32)
        for x in range(nx):
            cols = slice(x * wide, (x + 1) * wide)
            both = jnp.dot(main_matrix, stack[:, cols], preferred_element_type=F32)
            delta = both[:64] + both[64:] + rest[x * 64 : (x + 1) * 64]
            for y in range(ny):
                finish(x * ny + y, delta[:, y * LANES : (y + 1) * LANES])

    def outside(phase, out, scale):
        for f in range(4):
            pl.when(comes[f])(face_copy(kept, STEPS + 1, phase, 0, f, f ^ 1).wait_recv)
        rows = []
        for f in range(4):
            ref = (halo_x, halo_x, halo_y, halo_y)[f]
            blocks = [ref[phase, f % 2, i] for i in range(ref.shape[2])]
            blocks += [jnp.zeros((16, LANES), F32)] * (max(nx, ny) - len(blocks))
            high, low = halves(jnp.concatenate(blocks, axis=1))
            rows += [high, low, high]
        more_delta = jnp.dot(
            face_matrix, jnp.concatenate(rows, axis=0), preferred_element_type=F32
        )
        if scale != 1.0:
            more_delta = scale * more_delta
        sums = {}
        for f in range(4):
            for i in range((ny, ny, nx, nx)[f]):
                cell = (i, cells - ny + i, i * ny, i * ny + ny - 1)[f]
                part = more_delta[f * 64 : (f + 1) * 64, i * LANES : (i + 1) * LANES]
                sums[cell] = sums[cell] + part if cell in sums else part
        for cell, part in sums.items():
            out[cell] = out[cell] + part

    @pl.when(first)
    def _():
        load_init.wait()
        reorder(raw_start, fields.at[0])
        send_faces(fields.at[0], 0, 0, 0)

    load_state.wait()
    reorder(raw_state, kept)

    @pl.when(more)
    def _():
        send_faces(kept, STEPS + 1, 0, 1)

    load_force.wait()
    reorder(raw_force, source)

    load_volume.wait()
    load_lift.wait()
    row = lax.broadcasted_iota(jnp.int32, (64, 64), 0)
    column = lax.broadcasted_iota(jnp.int32, (64, 64), 1)
    weight = volume[...] - jnp.where(row == column, 0.1, 0.0).astype(F32)
    lifts = jnp.concatenate([lift[f] for f in range(6)], axis=0).T
    high, low = (half.astype(F32) for half in halves(jnp.concatenate([weight, lifts], axis=1)))

    def diagonal(blocks):
        rows, cols = blocks[0].shape
        return jnp.concatenate(
            [
                jnp.concatenate(
                    [block if i == j else jnp.zeros((rows, cols), F32) for j in range(len(blocks))], axis=1
                )
                for i, block in enumerate(blocks)
            ],
            axis=0,
        ).astype(BF16)

    main_matrix = jnp.concatenate(
        [
            jnp.concatenate([high, high[:, 64:]], axis=1),
            jnp.concatenate([low, jnp.zeros((64, 96), F32)], axis=1),
        ],
        axis=0,
    ).astype(BF16)
    low_matrix = diagonal([high[:, :64]] * nx)
    faces = [slice(64 + 16 * f, 80 + 16 * f) for f in range(4)]
    face_matrix = diagonal(
        [jnp.concatenate([high[:, at], high[:, at], low[:, at]], axis=1) for at in faces]
    )

    @pl.when(jnp.logical_not(first))
    def _():
        for x in range(nx):
            start_copy(x).wait_recv()
        reorder(raw_start, fields.at[0])

    for step in range(STEPS):
        now = fields.at[step]
        last = step == STEPS - 1
        out = resid if last else fields.at[step + 1]
        if step > 0:
            send_faces(now, step, step, 0)

        def finish(cell, delta, now=now, out=out, last=last):
            value = now[cell] + delta + source[cell]
            out[cell] = value - kept[cell] if last else value

        inside(now, finish)
        outside(step, out, 1.0)

    def err_copy(x):
        part = pl.ds(x * ny, ny)
        return pltpu.make_async_remote_copy(
            src_ref=error.at[part], dst_ref=earlier.at[part],
            send_sem=err_send.at[x], recv_sem=err_recv.at[x],
            device_id={"tm": tm + 1, "sx": sx, "sy": sy}, device_id_type=MESH,
        )

    @pl.when(first)
    def _():
        for cell in range(cells):
            error[cell] = resid[cell]

    @pl.when(jnp.logical_not(first))
    def _():
        for x in range(nx):
            err_copy(x).wait_recv()

        def finish(cell, delta):
            error[cell] = resid[cell] + earlier[cell] + 4.0 * delta

        inside(earlier, finish)
        outside(STEPS, error, 4.0)

    @pl.when(more)
    def _():
        send_faces(error, STEPS, STEPS, 1)
        for x in range(nx):
            err_copy(x).start()

    @pl.when(first)
    def _():
        sent_faces(fields.at[0], 0, 0, 0)

    for step in range(1, STEPS):
        sent_faces(fields.at[step], step, step, 0)

    @pl.when(more)
    def _():
        sent_faces(kept, STEPS + 1, 0, 1)
        for x in range(nx):
            start_copy(x).wait_send()
            err_copy(x).wait_send()
        sent_faces(error, STEPS, STEPS, 1)


def finishing(nx, ny, kept, resid, error, corr_hbm, resid_hbm, out_c, out_r, out_sem):
    cells = nx * ny
    copies = []
    for part in range(4):
        low, rows = part * 16 * cells, 16 * cells
        for cell in range(cells):
            dofs = slice(part * 16, part * 16 + 16)
            value = resid[cell, dofs, :]
            out_r[pl.ds(low + cell, 16, stride=cells), :] = value
            out_c[pl.ds(low + cell, 16, stride=cells), :] = kept[cell, dofs, :] + error[cell, dofs, :]
        for i, (src, dst) in enumerate(((out_r, resid_hbm), (out_c, corr_hbm))):
            span = pl.ds(low, rows)
            copies.append(pltpu.make_async_copy(src.at[span], dst.at[span], out_sem.at[part, i]))
            copies[-1].start()
    for copy in copies:
        copy.wait()


def solution(mesh):
    counts = tuple(mesh.shape[axis] for axis in ("tm", "sx", "sy"))

    def local(slices_state, forcing, initial, volume, lift):
        _, dofs, nx, ny, nz = slices_state.shape
        cells = nx * ny
        rows = dofs * cells
        raw = pltpu.VMEM((rows, nz), F32)
        field = pltpu.VMEM((cells, dofs, nz), F32)
        flat = jax.ShapeDtypeStruct((rows, nz), F32)
        shaped = jax.ShapeDtypeStruct((cells, dofs, nz), F32)
        vmem, hbm = pl.BlockSpec(memory_space=pltpu.VMEM), pl.BlockSpec(memory_space=pltpu.HBM)
        parts = pl.pallas_call(
            functools.partial(kernel, counts, nx, ny),
            out_shape=(shaped,) * 3,
            in_specs=[hbm] * 5,
            out_specs=(vmem,) * 3,
            scratch_shapes=[
                raw, raw, raw, pltpu.VMEM(volume.shape, F32), pltpu.VMEM((6, 16, dofs), F32),
                pltpu.VMEM((STEPS, cells, dofs, nz), F32), field, field,
                pltpu.VMEM((STEPS + 1, 2, ny, 16, nz), F32),
                pltpu.VMEM((STEPS + 1, 2, nx, 16, nz), F32),
                pltpu.VMEM((STEPS + 2, 2, nx, 16, nz), F32),
                pltpu.VMEM((256, cells * nz), BF16), pltpu.VMEM((dofs * nx, ny * nz), BF16),
                pltpu.SemaphoreType.DMA((5,)),
                pltpu.SemaphoreType.DMA((STEPS + 2, 4)),
                pltpu.SemaphoreType.DMA((STEPS + 1, 4)),
                pltpu.SemaphoreType.DMA((nx,)),
                pltpu.SemaphoreType.DMA((nx,)),
                pltpu.SemaphoreType.DMA((nx,)),
                pltpu.SemaphoreType.DMA((nx,)),
            ],
            compiler_params=pltpu.CompilerParams(
                collective_id=0, has_side_effects=True, vmem_limit_bytes=32 * 2**20
            ),
            name="cycle",
        )(
            *(
                pltpu.with_memory_space_constraint(value, pltpu.HBM)
                for value in (
                    slices_state.reshape(rows, nz), forcing.reshape(rows, nz),
                    initial.reshape(rows, nz), volume, jnp.swapaxes(lift, 1, 2),
                )
            )
        )
        corrected, residual = pl.pallas_call(
            functools.partial(finishing, nx, ny),
            out_shape=(flat,) * 2,
            in_specs=[vmem] * 3,
            out_specs=(hbm,) * 2,
            scratch_shapes=[raw, raw, pltpu.SemaphoreType.DMA((4, 2))],
            compiler_params=pltpu.CompilerParams(vmem_limit_bytes=16 * 2**20),
            name="finishing",
        )(*parts)
        shape = slices_state.shape
        return corrected.reshape(shape), residual.reshape(shape)

    split = P("tm", None, "sx", "sy", None)
    return jax.shard_map(
        local,
        mesh=mesh,
        in_specs=(split, split, P(None, "sx", "sy", None), P(), P()),
        out_specs=(split, split),
        check_vma=False,
    )
```

```python
import functools

import jax
import jax.numpy as jnp
from jax import lax
from jax.experimental import pallas as pl
from jax.experimental.pallas import tpu as pltpu
from jax.sharding import PartitionSpec as P

MESH = pl.DeviceIdType.MESH
F32, BF16 = jnp.float32, jnp.bfloat16
STEPS = 4
LANES = 128


def halves(value):
    high = value.astype(BF16)
    return high, (value - high.astype(F32)).astype(BF16)


def kernel(
    counts, nx, ny,
    state_hbm, force_hbm, init_hbm, vol_hbm, lift_hbm,
    kept, resid, error,
    raw_start, raw_state, raw_force, volume, lift,
    fields, source, earlier,
    halo_x, halo_y, sent_y, stack, lows,
    load_sem, face_send, face_recv, start_send, start_recv, err_send, err_recv,
):
    n_tm, n_sx, n_sy = counts
    cells = nx * ny
    tm, sx, sy = lax.axis_index("tm"), lax.axis_index("sx"), lax.axis_index("sy")
    first, more = tm == 0, tm < n_tm - 1
    exists = (sx < n_sx - 1, sx > 0, sy < n_sy - 1, sy > 0)
    comes = (sx > 0, sx < n_sx - 1, sy > 0, sy < n_sy - 1)
    shifts = ((1, 0), (-1, 0), (0, 1), (0, -1))

    def place(dt, f):
        dx, dy = shifts[f]
        return {"tm": tm + dt, "sx": sx + dx, "sy": sy + dy}

    barrier = pltpu.get_barrier_semaphore()

    def greet(dt, f):
        pl.semaphore_signal(barrier, inc=1, device_id=place(dt, f), device_id_type=MESH)

    for f in range(4):
        pl.when(exists[f])(functools.partial(greet, 0, f))
        pl.when(exists[f] & (tm > 0))(functools.partial(greet, -1, f))

    @pl.when(tm > 0)
    def _():
        pl.semaphore_signal(
            barrier, inc=1, device_id={"tm": tm - 1, "sx": sx, "sy": sy}, device_id_type=MESH
        )

    load_state = pltpu.make_async_copy(state_hbm, raw_state, load_sem.at[0])
    load_force = pltpu.make_async_copy(force_hbm, raw_force, load_sem.at[1])
    load_init = pltpu.make_async_copy(init_hbm, raw_start, load_sem.at[2])

    @pl.when(first)
    def _():
        load_init.start()

    load_state.start()
    load_force.start()
    load_volume = pltpu.make_async_copy(vol_hbm, volume, load_sem.at[3])
    load_lift = pltpu.make_async_copy(lift_hbm, lift, load_sem.at[4])
    load_volume.start()
    load_lift.start()

    wide, tall = ny * LANES, cells * LANES
    for shift in (0, 96):
        stack[64 + shift : 80 + shift, 0:wide] = jnp.zeros((16, wide), BF16)
        stack[80 + shift : 96 + shift, tall - wide : tall] = jnp.zeros((16, wide), BF16)
        for x in range(nx):
            left, right = x * wide, (x + 1) * wide
            stack[96 + shift : 112 + shift, left : left + LANES] = jnp.zeros((16, LANES), BF16)
            stack[112 + shift : 128 + shift, right - LANES : right] = jnp.zeros((16, LANES), BF16)

    def no_halo(f):
        ref = (halo_x, halo_x, halo_y, halo_y)[f]
        for phase in range(STEPS + 1):
            ref[phase, f % 2] = jnp.zeros(ref.shape[2:], F32)

    for f in range(4):
        pl.when(jnp.logical_not(comes[f]))(functools.partial(no_halo, f))

    total = sum(e.astype(jnp.int32) for e in exists)
    pl.semaphore_wait(barrier, total + jnp.where(more, total + 1, 0))

    def start_copy(x):
        part = pl.ds(x * 64 * ny, 64 * ny)
        return pltpu.make_async_remote_copy(
            src_ref=state_hbm.at[part], dst_ref=raw_start.at[part],
            send_sem=start_send.at[x], recv_sem=start_recv.at[x],
            device_id={"tm": tm + 1, "sx": sx, "sy": sy}, device_id_type=MESH,
        )

    @pl.when(more)
    def _():
        for x in range(nx):
            start_copy(x).start()

    top = lax.broadcasted_iota(jnp.int32, (8, LANES), 0) < 4
    lane = lax.broadcasted_iota(jnp.int32, (16, LANES), 1)

    def y_plus(ref, cell):
        parts = []
        for p in range(0, 64, 32):
            one, two = ref[cell, p + 8 : p + 16, :], ref[cell, p + 24 : p + 32, :]
            parts.append(jnp.where(top, pltpu.roll(one, 4, 0), two))
        return jnp.concatenate(parts, axis=0)

    def y_minus(ref, cell):
        parts = []
        for p in range(0, 64, 32):
            one, two = ref[cell, p : p + 8, :], ref[cell, p + 16 : p + 24, :]
            parts.append(jnp.where(top, one, pltpu.roll(two, 4, 0)))
        return jnp.concatenate(parts, axis=0)

    def face_copy(ref, slot, phase, dt, f, to=None):
        if f == 0:
            src = ref.at[pl.ds(cells - ny, ny), pl.ds(48, 16), :]
        elif f == 1:
            src = ref.at[pl.ds(0, ny), pl.ds(0, 16), :]
        else:
            src = sent_y.at[slot, f - 2]
        target = (halo_x, halo_x, halo_y, halo_y)[f].at[phase, f % 2]
        return pltpu.make_async_remote_copy(
            src_ref=src, dst_ref=target,
            send_sem=face_send.at[dt, f], recv_sem=face_recv.at[phase, f],
            device_id=place(dt, f if to is None else to), device_id_type=MESH,
        )

    def send_faces(ref, slot, phase, dt):
        odd = lax.rem(sx, 2) == 1
        pl.when(exists[0] & odd)(face_copy(ref, slot, phase, dt, 0).start)
        pl.when(exists[1])(face_copy(ref, slot, phase, dt, 1).start)
        pl.when(exists[0] & jnp.logical_not(odd))(face_copy(ref, slot, phase, dt, 0).start)
        for x in range(nx):
            sent_y[slot, 0, x] = y_plus(ref, x * ny + ny - 1)
            sent_y[slot, 1, x] = y_minus(ref, x * ny)
        for f in range(2, 4):
            pl.when(exists[f])(face_copy(ref, slot, phase, dt, f).start)

    def sent_faces(dt, phases):
        for f in range(4):
            block = (halo_x, halo_x, halo_y, halo_y)[f].at[pl.ds(0, phases), f % 2]
            copy = pltpu.make_async_remote_copy(
                src_ref=block, dst_ref=block, send_sem=face_send.at[dt, f], recv_sem=face_recv.at[0, f],
                device_id=place(dt, f), device_id_type=MESH,
            )
            pl.when(exists[f])(copy.wait_send)

    def reorder(raw, ref):
        for cell in range(cells):
            ref[cell] = raw[pl.ds(cell, 64, stride=cells), :]

    def inside(ref, finish):
        def put(rows, cell, pair):
            cols = slice(cell * LANES, (cell + 1) * LANES)
            stack[rows : rows + 16, cols] = pair[0]
            stack[rows + 96 : rows + 112, cols] = pair[1]

        for x in range(nx):
            for y in range(ny):
                cell = x * ny + y
                high, low = halves(ref[cell])
                stack[0:64, cell * LANES : (cell + 1) * LANES] = high
                lows[x * 64 : (x + 1) * 64, y * LANES : (y + 1) * LANES] = low
                if x + 1 < nx:
                    put(64, cell + ny, (high[48:64], low[48:64]))
                if x > 0:
                    put(80, cell - ny, (high[0:16], low[0:16]))
                if y + 1 < ny:
                    put(96, cell + 1, halves(y_plus(ref, cell)))
                if y > 0:
                    put(112, cell - 1, halves(y_minus(ref, cell)))
                up = pltpu.roll(ref[cell, pl.ds(3, 16, stride=4), :], 1, 1)
                put(128, cell, halves(jnp.where(lane == 0, 0.0, up)))
                down = pltpu.roll(ref[cell, pl.ds(0, 16, stride=4), :], LANES - 1, 1)
                put(144, cell, halves(jnp.where(lane == LANES - 1, 0.0, down)))
        rest = jnp.dot(low_matrix, lows[...], preferred_element_type=F32)
        for x in range(nx):
            cols = slice(x * wide, (x + 1) * wide)
            both = jnp.dot(main_matrix, stack[:, cols], preferred_element_type=F32)
            delta = both[:64] + both[64:] + rest[x * 64 : (x + 1) * 64]
            for y in range(ny):
                finish(x * ny + y, delta[:, y * LANES : (y + 1) * LANES])

    def outside(phase, out, scale):
        for f in range(4):
            pl.when(comes[f])(face_copy(kept, STEPS + 1, phase, 0, f, f ^ 1).wait_recv)
        rows = []
        for f in range(4):
            ref = (halo_x, halo_x, halo_y, halo_y)[f]
            blocks = [ref[phase, f % 2, i] for i in range(ref.shape[2])]
            blocks += [jnp.zeros((16, LANES), F32)] * (max(nx, ny) - len(blocks))
            high, low = halves(jnp.concatenate(blocks, axis=1))
            rows += [high, low, high]
        more_delta = jnp.dot(
            face_matrix, jnp.concatenate(rows, axis=0), preferred_element_type=F32
        )
        if scale != 1.0:
            more_delta = scale * more_delta
        sums = {}
        for f in range(4):
            for i in range((ny, ny, nx, nx)[f]):
                cell = (i, cells - ny + i, i * ny, i * ny + ny - 1)[f]
                part = more_delta[f * 64 : (f + 1) * 64, i * LANES : (i + 1) * LANES]
                sums[cell] = sums[cell] + part if cell in sums else part
        for cell, part in sums.items():
            out[cell] = out[cell] + part

    @pl.when(first)
    def _():
        load_init.wait()
        reorder(raw_start, fields.at[0])
        send_faces(fields.at[0], 0, 0, 0)

    load_state.wait()
    reorder(raw_state, kept)

    @pl.when(more)
    def _():
        send_faces(kept, STEPS + 1, 0, 1)

    load_force.wait()
    reorder(raw_force, source)

    load_volume.wait()
    load_lift.wait()
    row = lax.broadcasted_iota(jnp.int32, (64, 64), 0)
    column = lax.broadcasted_iota(jnp.int32, (64, 64), 1)
    weight = volume[...] - jnp.where(row == column, 0.1, 0.0).astype(F32)
    lifts = jnp.concatenate([lift[f] for f in range(6)], axis=0).T
    high, low = (half.astype(F32) for half in halves(jnp.concatenate([weight, lifts], axis=1)))

    def diagonal(blocks):
        rows, cols = blocks[0].shape
        return jnp.concatenate(
            [
                jnp.concatenate(
                    [block if i == j else jnp.zeros((rows, cols), F32) for j in range(len(blocks))], axis=1
                )
                for i, block in enumerate(blocks)
            ],
            axis=0,
        ).astype(BF16)

    main_matrix = jnp.concatenate(
        [
            jnp.concatenate([high, high[:, 64:]], axis=1),
            jnp.concatenate([low, jnp.zeros((64, 96), F32)], axis=1),
        ],
        axis=0,
    ).astype(BF16)
    low_matrix = diagonal([high[:, :64]] * nx)
    faces = [slice(64 + 16 * f, 80 + 16 * f) for f in range(4)]
    face_matrix = diagonal(
        [jnp.concatenate([high[:, at], high[:, at], low[:, at]], axis=1) for at in faces]
    )

    @pl.when(jnp.logical_not(first))
    def _():
        for x in range(nx):
            start_copy(x).wait_recv()
        reorder(raw_start, fields.at[0])

    early = [(x * ny + 1, ny - 2) for x in range(1, nx - 1)] if ny > 2 else []
    marks = [0] + [edge for start, size in early for edge in (start, start + size)] + [cells]
    late = [(low, high - low) for low, high in zip(marks[::2], marks[1::2])]

    def err_copy(part, ref):
        at = pl.ds(*part)
        index = (early + late).index(part)
        return pltpu.make_async_remote_copy(
            src_ref=ref.at[at], dst_ref=earlier.at[at],
            send_sem=err_send.at[index], recv_sem=err_recv.at[index],
            device_id={"tm": tm + 1, "sx": sx, "sy": sy}, device_id_type=MESH,
        )

    def send_early(ref):
        @pl.when(more)
        def _():
            for part in early:
                err_copy(part, ref).start()

    def send_late(ref):
        @pl.when(more)
        def _():
            send_faces(ref, STEPS, STEPS, 1)
            for part in late:
                err_copy(part, ref).start()

    for step in range(STEPS):
        now = fields.at[step]
        last = step == STEPS - 1
        out = resid if last else fields.at[step + 1]
        if step > 0:
            send_faces(now, step, step, 0)

        def finish(cell, delta, now=now, out=out, last=last):
            value = now[cell] + delta + source[cell]
            out[cell] = value - kept[cell] if last else value

        inside(now, finish)
        if last:
            pl.when(first)(functools.partial(send_early, resid))
        outside(step, out, 1.0)

    @pl.when(first)
    def _():
        send_late(resid)
        for cell in range(cells):
            error[cell] = resid[cell]
        sent_faces(0, STEPS)

    @pl.when(jnp.logical_not(first))
    def _():
        sent_faces(0, STEPS - 1)
        for part in early + late:
            err_copy(part, error).wait_recv()

        def finish(cell, delta):
            error[cell] = resid[cell] + earlier[cell] + 4.0 * delta

        inside(earlier, finish)
        send_early(error)
        outside(STEPS, error, 4.0)
        send_late(error)

    @pl.when(more)
    def _():
        for x in range(nx):
            start_copy(x).wait_send()
        for part in early + late:
            err_copy(part, resid).wait_send()
        sent_faces(1, 2)


def finishing(nx, ny, kept, resid, error, corr_hbm, resid_hbm, out_c, out_r, out_sem):
    cells = nx * ny
    copies = []
    for part in range(4):
        low, rows = part * 16 * cells, 16 * cells
        for cell in range(cells):
            dofs = slice(part * 16, part * 16 + 16)
            value = resid[cell, dofs, :]
            out_r[pl.ds(low + cell, 16, stride=cells), :] = value
            out_c[pl.ds(low + cell, 16, stride=cells), :] = kept[cell, dofs, :] + error[cell, dofs, :]
        for i, (src, dst) in enumerate(((out_r, resid_hbm), (out_c, corr_hbm))):
            span = pl.ds(low, rows)
            copies.append(pltpu.make_async_copy(src.at[span], dst.at[span], out_sem.at[part, i]))
            copies[-1].start()
    for copy in copies:
        copy.wait()


def solution(mesh):
    counts = tuple(mesh.shape[axis] for axis in ("tm", "sx", "sy"))

    def local(slices_state, forcing, initial, volume, lift):
        _, dofs, nx, ny, nz = slices_state.shape
        cells = nx * ny
        rows = dofs * cells
        raw = pltpu.VMEM((rows, nz), F32)
        field = pltpu.VMEM((cells, dofs, nz), F32)
        flat = jax.ShapeDtypeStruct((rows, nz), F32)
        shaped = jax.ShapeDtypeStruct((cells, dofs, nz), F32)
        vmem, hbm = pl.BlockSpec(memory_space=pltpu.VMEM), pl.BlockSpec(memory_space=pltpu.HBM)
        parts = pl.pallas_call(
            functools.partial(kernel, counts, nx, ny),
            out_shape=(shaped,) * 3,
            in_specs=[hbm] * 5,
            out_specs=(vmem,) * 3,
            scratch_shapes=[
                raw, raw, raw, pltpu.VMEM(volume.shape, F32), pltpu.VMEM((6, 16, dofs), F32),
                pltpu.VMEM((STEPS, cells, dofs, nz), F32), field, field,
                pltpu.VMEM((STEPS + 1, 2, ny, 16, nz), F32),
                pltpu.VMEM((STEPS + 1, 2, nx, 16, nz), F32),
                pltpu.VMEM((STEPS + 2, 2, nx, 16, nz), F32),
                pltpu.VMEM((256, cells * nz), BF16), pltpu.VMEM((dofs * nx, ny * nz), BF16),
                pltpu.SemaphoreType.DMA((5,)),
                pltpu.SemaphoreType.DMA((2, 4)),
                pltpu.SemaphoreType.DMA((STEPS + 1, 4)),
                pltpu.SemaphoreType.DMA((nx,)),
                pltpu.SemaphoreType.DMA((nx,)),
                pltpu.SemaphoreType.DMA((2 * nx,)),
                pltpu.SemaphoreType.DMA((2 * nx,)),
            ],
            compiler_params=pltpu.CompilerParams(
                collective_id=0, has_side_effects=True, vmem_limit_bytes=32 * 2**20
            ),
            name="cycle",
        )(
            *(
                pltpu.with_memory_space_constraint(value, pltpu.HBM)
                for value in (
                    slices_state.reshape(rows, nz), forcing.reshape(rows, nz),
                    initial.reshape(rows, nz), volume, jnp.swapaxes(lift, 1, 2),
                )
            )
        )
        corrected, residual = pl.pallas_call(
            functools.partial(finishing, nx, ny),
            out_shape=(flat,) * 2,
            in_specs=[vmem] * 3,
            out_specs=(hbm,) * 2,
            scratch_shapes=[raw, raw, pltpu.SemaphoreType.DMA((4, 2))],
            compiler_params=pltpu.CompilerParams(vmem_limit_bytes=16 * 2**20),
            name="finishing",
        )(*parts)
        shape = slices_state.shape
        return corrected.reshape(shape), residual.reshape(shape)

    split = P("tm", None, "sx", "sy", None)
    return jax.shard_map(
        local,
        mesh=mesh,
        in_specs=(split, split, P(None, "sx", "sy", None), P(), P()),
        out_specs=(split, split),
        check_vma=False,
    )
```

```python
import functools

import jax
import jax.numpy as jnp
from jax import lax
from jax.experimental import pallas as pl
from jax.experimental.pallas import tpu as pltpu
from jax.sharding import PartitionSpec as P

MESH = pl.DeviceIdType.MESH
F32, BF16 = jnp.float32, jnp.bfloat16
STEPS = 4
WHOLE = (0, 2, 4)
PAIRED = (0, 2)
LANES = 128


def halves(value):
    high = value.astype(BF16)
    return high, (value - high.astype(F32)).astype(BF16)


def kernel(
    counts, nx, ny,
    state_hbm, force_hbm, init_hbm, vol_hbm, lift_hbm,
    kept, resid, error,
    raw_start, raw_state, raw_force, volume, lift,
    fields, source, earlier,
    halo_x, halo_y, sent_y, corner, edge, sent_edge, edge_y, sent_edge_y, s_high, s_low,
    load_sem, face_send, face_recv, start_send, start_recv, err_send, err_recv,
    corner_send, corner_recv, edge_send, edge_recv,
):
    n_tm, n_sx, n_sy = counts
    cells = nx * ny
    tm, sx, sy = lax.axis_index("tm"), lax.axis_index("sx"), lax.axis_index("sy")
    first, more = tm == 0, tm < n_tm - 1
    exists = (sx < n_sx - 1, sx > 0, sy < n_sy - 1, sy > 0)
    comes = (sx > 0, sx < n_sx - 1, sy > 0, sy < n_sy - 1)
    shifts = ((1, 0), (-1, 0), (0, 1), (0, -1))
    diagonals = [(fx, fy) for fx in (0, 1) for fy in (2, 3)]

    def place(dt, f):
        dx, dy = shifts[f]
        return {"tm": tm + dt, "sx": sx + dx, "sy": sy + dy}

    def across(dt, fx, fy):
        return {"tm": tm + dt, "sx": sx + shifts[fx][0], "sy": sy + shifts[fy][1]}

    load_state = pltpu.make_async_copy(state_hbm, raw_state, load_sem.at[0])
    load_force = pltpu.make_async_copy(force_hbm, raw_force, load_sem.at[1])
    load_init = pltpu.make_async_copy(init_hbm, raw_start, load_sem.at[2])

    @pl.when(first)
    def _():
        load_init.start()

    load_state.start()
    load_force.start()
    load_volume = pltpu.make_async_copy(vol_hbm, volume, load_sem.at[3])
    load_lift = pltpu.make_async_copy(lift_hbm, lift, load_sem.at[4])
    load_volume.start()
    load_lift.start()

    barrier = pltpu.get_barrier_semaphore()

    def greet(dt, f):
        pl.semaphore_signal(barrier, inc=1, device_id=place(dt, f), device_id_type=MESH)

    for f in range(4):
        pl.when(exists[f])(functools.partial(greet, 0, f))
        pl.when(exists[f] & (tm > 0))(functools.partial(greet, -1, f))

    def greet_across(dt, fx, fy):
        pl.semaphore_signal(
            barrier, inc=1, device_id=across(dt, fx, fy), device_id_type=MESH
        )

    for fx, fy in diagonals:
        there = exists[fx] & exists[fy]
        pl.when(there)(functools.partial(greet_across, 0, fx, fy))
        pl.when(there & (tm > 0))(functools.partial(greet_across, -1, fx, fy))

    @pl.when(tm > 0)
    def _():
        pl.semaphore_signal(
            barrier, inc=1, device_id={"tm": tm - 1, "sx": sx, "sy": sy}, device_id_type=MESH
        )

    wide, tall = ny * LANES, cells * LANES
    for stack in (s_high, s_low):
        stack[64:80, 0:wide] = jnp.zeros((16, wide), BF16)
        stack[80:96, tall - wide : tall] = jnp.zeros((16, wide), BF16)
        for x in range(nx):
            low, high = x * wide, (x + 1) * wide
            stack[96:112, low : low + LANES] = jnp.zeros((16, LANES), BF16)
            stack[112:128, high - LANES : high] = jnp.zeros((16, LANES), BF16)

    def no_halo(f):
        ref = (halo_x, halo_x, halo_y, halo_y)[f]
        for phase in range(STEPS + 1):
            ref[phase, f % 2] = jnp.zeros(ref.shape[2:], F32)

    for f in range(4):
        pl.when(jnp.logical_not(comes[f]))(functools.partial(no_halo, f))

    def no_corner(fx, fy):
        for pair in range(STEPS // 2):
            for kind in range(2):
                corner[kind, pair, fx, fy - 2] = jnp.zeros((16, LANES), F32)

    for fx, fy in diagonals:
        pl.when(jnp.logical_not(comes[fx] & comes[fy]))(functools.partial(no_corner, fx, fy))

    total = sum(e.astype(jnp.int32) for e in exists)
    total = total + sum((exists[fx] & exists[fy]).astype(jnp.int32) for fx, fy in diagonals)
    pl.semaphore_wait(barrier, total + jnp.where(more, total + 1, 0))

    def start_copy(x):
        part = pl.ds(x * 64 * ny, 64 * ny)
        return pltpu.make_async_remote_copy(
            src_ref=state_hbm.at[part], dst_ref=raw_start.at[part],
            send_sem=start_send.at[x], recv_sem=start_recv.at[x],
            device_id={"tm": tm + 1, "sx": sx, "sy": sy}, device_id_type=MESH,
        )

    @pl.when(more)
    def _():
        for x in range(nx):
            start_copy(x).start()

    top = lax.broadcasted_iota(jnp.int32, (8, LANES), 0) < 4
    lane = lax.broadcasted_iota(jnp.int32, (16, LANES), 1)

    def y_plus(ref, cell):
        parts = []
        for p in range(0, 64, 32):
            one, two = ref[cell, p + 8 : p + 16, :], ref[cell, p + 24 : p + 32, :]
            parts.append(jnp.where(top, pltpu.roll(one, 4, 0), two))
        return jnp.concatenate(parts, axis=0)

    def y_minus(ref, cell):
        parts = []
        for p in range(0, 64, 32):
            one, two = ref[cell, p : p + 8, :], ref[cell, p + 16 : p + 24, :]
            parts.append(jnp.where(top, one, pltpu.roll(two, 4, 0)))
        return jnp.concatenate(parts, axis=0)

    def face_copy(ref, slot, phase, dt, f, to=None):
        if f == 0:
            src = ref.at[pl.ds(cells - ny, ny), pl.ds(48, 16), :]
        elif f == 1:
            src = ref.at[pl.ds(0, ny), pl.ds(0, 16), :]
        else:
            src = sent_y.at[slot, f - 2]
        target = (halo_x, halo_x, halo_y, halo_y)[f].at[phase, f % 2]
        return pltpu.make_async_remote_copy(
            src_ref=src, dst_ref=target,
            send_sem=face_send.at[slot, f], recv_sem=face_recv.at[phase, f],
            device_id=place(dt, f if to is None else to), device_id_type=MESH,
        )

    def send_faces(ref, slot, phase, dt):
        if phase in WHOLE:
            odd = lax.rem(sx, 2) == 1
            pl.when(exists[0] & odd)(face_copy(ref, slot, phase, dt, 0).start)
            pl.when(exists[1])(face_copy(ref, slot, phase, dt, 1).start)
            pl.when(exists[0] & jnp.logical_not(odd))(face_copy(ref, slot, phase, dt, 0).start)
        for x in range(nx):
            sent_y[slot, 0, x] = y_plus(ref, x * ny + ny - 1)
            sent_y[slot, 1, x] = y_minus(ref, x * ny)
        for f in range(2, 4):
            pl.when(exists[f])(face_copy(ref, slot, phase, dt, f).start)
        if phase in PAIRED:
            for fx, fy in diagonals:
                for kind in range(2):
                    copy = corner_copy(ref, slot, phase, dt, fx, fy, kind)
                    pl.when(exists[fx] & exists[fy])(copy.start)

    def sent_faces(ref, slot, phase, dt):
        for f in range(4) if phase in WHOLE else range(2, 4):
            pl.when(exists[f])(face_copy(ref, slot, phase, dt, f).wait_send)
        if phase in PAIRED:
            for fx, fy in diagonals:
                for kind in range(2):
                    copy = corner_copy(ref, slot, phase, dt, fx, fy, kind)
                    pl.when(exists[fx] & exists[fy])(copy.wait_send)

    def corner_copy(ref, slot, phase, dt, fx, fy, kind, back=False):
        x, y = (nx - 1 if fx == 0 else 0), (ny - 1 if fy == 2 else 0)
        pair, index = PAIRED.index(phase), 2 * fx + fy - 2
        if kind == 0:
            src = sent_y.at[slot, fy - 2, x]
        else:
            src = ref.at[x * ny + y, pl.ds(48 if fx == 0 else 0, 16), :]
        target = across(dt, fx ^ 1, fy ^ 1) if back else across(dt, fx, fy)
        return pltpu.make_async_remote_copy(
            src_ref=src, dst_ref=corner.at[kind, pair, fx, fy - 2],
            send_sem=corner_send.at[kind, slot, index], recv_sem=corner_recv.at[kind, pair, index],
            device_id=target, device_id_type=MESH,
        )

    def edge_copy(pair, f, to=None):
        src, dst = ((sent_edge, edge), (sent_edge_y, edge_y))[f // 2]
        return pltpu.make_async_remote_copy(
            src_ref=src.at[pair, f % 2], dst_ref=dst.at[pair, f % 2],
            send_sem=edge_send.at[pair, f], recv_sem=edge_recv.at[pair, f],
            device_id=place(0, f if to is None else to), device_id_type=MESH,
        )

    def send_edges(pair, ref):
        for y in range(ny):
            sent_edge[pair, 0, y] = ref[cells - ny + y, 48:64, :]
            sent_edge[pair, 1, y] = ref[y, 0:16, :]
        for f in range(2):
            pl.when(exists[f])(edge_copy(pair, f).start)

    def send_edges_y(pair, ref):
        for x in range(nx):
            sent_edge_y[pair, 0, x] = y_plus(ref, x * ny + ny - 1)
            sent_edge_y[pair, 1, x] = y_minus(ref, x * ny)
        for f in range(2, 4):
            pl.when(exists[f])(edge_copy(pair, f).start)

    def next_faces(phase):
        pair, now = PAIRED.index(phase), fields.at[phase]
        for f in range(4):

            @pl.when(comes[f])
            def _(f=f):
                edge_copy(pair, f, f ^ 1).wait_recv()
                sides = (2, 3) if f < 2 else (0, 1)
                found = []
                for g in sides:
                    fx, fy = (f, g) if f < 2 else (g, f)
                    back = corner_copy(now, 0, phase, 0, fx, fy, f // 2, True)
                    pl.when(comes[g])(back.wait_recv)
                    found.append(corner[f // 2, pair, fx, fy - 2])
                if f < 2:
                    count, kept_edge, halo = ny, edge, halo_x
                    cell, low = (0, 0) if f == 0 else (cells - ny, 48)
                    own = [now[cell + y, low : low + 16, :] for y in range(ny)]
                else:
                    count, kept_edge, halo = nx, edge_y, halo_y
                    own = [
                        y_minus(now, x * ny) if f == 2 else y_plus(now, x * ny + ny - 1) for x in range(nx)
                    ]
                none = [jnp.zeros((16, LANES), F32)] * (count - 1)
                rows = []
                for blocks in (own, [found[0]] + none, none + [found[1]]):
                    high, part = halves(jnp.concatenate(blocks, axis=1))
                    rows += [high, part, high]
                added = jnp.dot(
                    edge_matrix[f], jnp.concatenate(rows, axis=0), preferred_element_type=F32
                )
                for i in range(count):
                    halo[phase + 1, f % 2, i] = (
                        kept_edge[pair, f % 2, i] + added[:, i * LANES : (i + 1) * LANES]
                    )

    def reorder(raw, ref):
        for cell in range(cells):
            ref[cell] = raw[pl.ds(cell, 64, stride=cells), :]

    def inside(ref, finish, edges=None):
        def put(rows, cell, value):
            high, low = halves(value)
            cols = slice(cell * LANES, (cell + 1) * LANES)
            s_high[rows : rows + value.shape[0], cols] = high
            s_low[rows : rows + value.shape[0], cols] = low

        for x in range(nx):
            for y in range(ny):
                cell = x * ny + y
                pair = halves(ref[cell])
                for stack, half in zip((s_high, s_low), pair):
                    stack[0:64, cell * LANES : (cell + 1) * LANES] = half
                    if x + 1 < nx:
                        stack[64:80, (cell + ny) * LANES : (cell + ny + 1) * LANES] = half[48:64]
                    if x > 0:
                        stack[80:96, (cell - ny) * LANES : (cell - ny + 1) * LANES] = half[0:16]
                if y + 1 < ny:
                    put(96, cell + 1, y_plus(ref, cell))
                if y > 0:
                    put(112, cell - 1, y_minus(ref, cell))
                up = pltpu.roll(ref[cell, pl.ds(3, 16, stride=4), :], 1, 1)
                put(128, cell, jnp.where(lane == 0, 0.0, up))
                down = pltpu.roll(ref[cell, pl.ds(0, 16, stride=4), :], LANES - 1, 1)
                put(144, cell, jnp.where(lane == LANES - 1, 0.0, down))
        order = list(dict.fromkeys([0, nx - 1] + list(range(nx))))
        for turn, x in enumerate(order):
            if edges is not None and turn == min(2, nx):
                edges()
            cols = slice(x * wide, (x + 1) * wide)
            both = jnp.dot(a_both, s_high[:, cols], preferred_element_type=F32)
            rest = jnp.dot(a_high, s_low[:, cols], preferred_element_type=F32)
            delta = both[:64] + both[64:] + rest
            for y in range(ny):
                finish(x * ny + y, delta[:, y * LANES : (y + 1) * LANES])

    def outside(phase, out, scale):
        for faces in ((2, 3), (0, 1)):
            for f in faces:
                if phase not in WHOLE:
                    continue
                pl.when(comes[f])(face_copy(kept, STEPS + 1, phase, 0, f, f ^ 1).wait_recv)
            for f in faces:
                ref = (halo_x, halo_x, halo_y, halo_y)[f]
                count = ref.shape[2]
                trace = jnp.concatenate([ref[phase, f % 2, i] for i in range(count)], axis=1)
                high, low = halves(trace)
                added = jnp.dot(
                    face_matrix[f], jnp.concatenate([high, low, high], axis=0), preferred_element_type=F32
                )
                if scale != 1.0:
                    added = scale * added
                for i in range(count):
                    cell = (i, cells - ny + i, i * ny, i * ny + ny - 1)[f]
                    out[cell] = out[cell] + added[:, i * LANES : (i + 1) * LANES]

    @pl.when(first)
    def _():
        load_init.wait()
        reorder(raw_start, fields.at[0])
        send_faces(fields.at[0], 0, 0, 0)

    load_state.wait()
    reorder(raw_state, kept)

    @pl.when(more)
    def _():
        send_faces(kept, STEPS + 1, 0, 1)

    load_force.wait()
    reorder(raw_force, source)

    load_volume.wait()
    load_lift.wait()
    row = lax.broadcasted_iota(jnp.int32, (64, 64), 0)
    column = lax.broadcasted_iota(jnp.int32, (64, 64), 1)
    weight = volume[...] - jnp.where(row == column, 0.1, 0.0).astype(F32)
    lifts = jnp.concatenate([lift[f] for f in range(6)], axis=0).T
    a_high, a_low = halves(jnp.concatenate([weight, lifts], axis=1))
    a_both = jnp.concatenate([a_high, a_low], axis=0)
    thirds = []
    for f in range(4):
        high, low = halves(lifts[:, 16 * f : 16 * f + 16])
        thirds.append(jnp.concatenate([high.astype(F32), high.astype(F32), low.astype(F32)], axis=1))
    face_matrix = [third.astype(BF16) for third in thirds]
    edge_matrix = []
    for f in range(4):
        picked = []
        for g in (f ^ 1,) + ((2, 3) if f < 2 else (0, 1)):
            third = thirds[g]
            if f < 2:
                picked.append(third[48:64] if f == 0 else third[0:16])
            else:
                low = 12 if f == 2 else 0
                picked.append(jnp.concatenate([third[p + low : p + low + 4] for p in range(0, 64, 16)], axis=0))
        edge_matrix.append(jnp.concatenate(picked, axis=1).astype(BF16))

    @pl.when(jnp.logical_not(first))
    def _():
        for x in range(nx):
            start_copy(x).wait_recv()
        reorder(raw_start, fields.at[0])

    for step in range(STEPS):
        now = fields.at[step]
        last = step == STEPS - 1
        out = resid if last else fields.at[step + 1]
        if step > 0 and step in WHOLE:
            send_faces(now, step, step, 0)

        def finish(cell, delta, now=now, out=out, last=last):
            value = now[cell] + delta + source[cell]
            out[cell] = value - kept[cell] if last else value

        if step in PAIRED:
            inside(now, finish, functools.partial(send_edges, PAIRED.index(step), out))
            send_edges_y(PAIRED.index(step), out)
        else:
            inside(now, finish)
            next_faces(step - 1)
        outside(step, out, 1.0)

    def err_copy(x):
        part = pl.ds(x * ny, ny)
        return pltpu.make_async_remote_copy(
            src_ref=error.at[part], dst_ref=earlier.at[part],
            send_sem=err_send.at[x], recv_sem=err_recv.at[x],
            device_id={"tm": tm + 1, "sx": sx, "sy": sy}, device_id_type=MESH,
        )

    @pl.when(first)
    def _():
        for cell in range(cells):
            error[cell] = resid[cell]

    @pl.when(jnp.logical_not(first))
    def _():
        for x in range(nx):
            err_copy(x).wait_recv()

        def finish(cell, delta):
            error[cell] = resid[cell] + earlier[cell] + 4.0 * delta

        inside(earlier, finish)
        outside(STEPS, error, 4.0)

    @pl.when(more)
    def _():
        send_faces(error, STEPS, STEPS, 1)
        for x in range(nx):
            err_copy(x).start()

    @pl.when(first)
    def _():
        sent_faces(fields.at[0], 0, 0, 0)

    for step in WHOLE[1:-1]:
        sent_faces(fields.at[step], step, step, 0)
    for pair in range(len(PAIRED)):
        for f in range(4):
            pl.when(exists[f])(edge_copy(pair, f).wait_send)

    @pl.when(more)
    def _():
        sent_faces(kept, STEPS + 1, 0, 1)
        for x in range(nx):
            start_copy(x).wait_send()
            err_copy(x).wait_send()
        sent_faces(error, STEPS, STEPS, 1)


def finishing(nx, ny, kept, resid, error, corr_hbm, resid_hbm, out_c, out_r, out_sem):
    cells = nx * ny
    copies = []
    for part in range(4):
        low, rows = part * 16 * cells, 16 * cells
        for cell in range(cells):
            dofs = slice(part * 16, part * 16 + 16)
            value = resid[cell, dofs, :]
            out_r[pl.ds(low + cell, 16, stride=cells), :] = value
            out_c[pl.ds(low + cell, 16, stride=cells), :] = kept[cell, dofs, :] + error[cell, dofs, :]
        for i, (src, dst) in enumerate(((out_r, resid_hbm), (out_c, corr_hbm))):
            span = pl.ds(low, rows)
            copies.append(pltpu.make_async_copy(src.at[span], dst.at[span], out_sem.at[part, i]))
            copies[-1].start()
    for copy in copies:
        copy.wait()


def solution(mesh):
    counts = tuple(mesh.shape[axis] for axis in ("tm", "sx", "sy"))

    def local(slices_state, forcing, initial, volume, lift):
        _, dofs, nx, ny, nz = slices_state.shape
        cells = nx * ny
        rows = dofs * cells
        raw = pltpu.VMEM((rows, nz), F32)
        field = pltpu.VMEM((cells, dofs, nz), F32)
        stack = pltpu.VMEM((160, cells * nz), BF16)
        flat = jax.ShapeDtypeStruct((rows, nz), F32)
        shaped = jax.ShapeDtypeStruct((cells, dofs, nz), F32)
        vmem, hbm = pl.BlockSpec(memory_space=pltpu.VMEM), pl.BlockSpec(memory_space=pltpu.HBM)
        parts = pl.pallas_call(
            functools.partial(kernel, counts, nx, ny),
            out_shape=(shaped,) * 3,
            in_specs=[hbm] * 5,
            out_specs=(vmem,) * 3,
            scratch_shapes=[
                raw, raw, raw, pltpu.VMEM(volume.shape, F32), pltpu.VMEM((6, 16, dofs), F32),
                pltpu.VMEM((STEPS, cells, dofs, nz), F32), field, field,
                pltpu.VMEM((STEPS + 1, 2, ny, 16, nz), F32),
                pltpu.VMEM((STEPS + 1, 2, nx, 16, nz), F32),
                pltpu.VMEM((STEPS + 2, 2, nx, 16, nz), F32),
                pltpu.VMEM((2, STEPS // 2, 2, 2, 16, nz), F32),
                pltpu.VMEM((STEPS // 2, 2, ny, 16, nz), F32),
                pltpu.VMEM((STEPS // 2, 2, ny, 16, nz), F32),
                pltpu.VMEM((STEPS // 2, 2, nx, 16, nz), F32),
                pltpu.VMEM((STEPS // 2, 2, nx, 16, nz), F32),
                stack, stack,
                pltpu.SemaphoreType.DMA((5,)),
                pltpu.SemaphoreType.DMA((STEPS + 2, 4)),
                pltpu.SemaphoreType.DMA((STEPS + 1, 4)),
                pltpu.SemaphoreType.DMA((nx,)),
                pltpu.SemaphoreType.DMA((nx,)),
                pltpu.SemaphoreType.DMA((nx,)),
                pltpu.SemaphoreType.DMA((nx,)),
                pltpu.SemaphoreType.DMA((2, STEPS + 2, 4)),
                pltpu.SemaphoreType.DMA((2, STEPS // 2, 4)),
                pltpu.SemaphoreType.DMA((STEPS // 2, 4)),
                pltpu.SemaphoreType.DMA((STEPS // 2, 4)),
            ],
            compiler_params=pltpu.CompilerParams(
                collective_id=0, has_side_effects=True, vmem_limit_bytes=32 * 2**20
            ),
            name="cycle",
        )(
            *(
                pltpu.with_memory_space_constraint(value, pltpu.HBM)
                for value in (
                    slices_state.reshape(rows, nz), forcing.reshape(rows, nz),
                    initial.reshape(rows, nz), volume, jnp.swapaxes(lift, 1, 2),
                )
            )
        )
        corrected, residual = pl.pallas_call(
            functools.partial(finishing, nx, ny),
            out_shape=(flat,) * 2,
            in_specs=[vmem] * 3,
            out_specs=(hbm,) * 2,
            scratch_shapes=[raw, raw, pltpu.SemaphoreType.DMA((4, 2))],
            compiler_params=pltpu.CompilerParams(vmem_limit_bytes=16 * 2**20),
            name="finishing",
        )(*parts)
        shape = slices_state.shape
        return corrected.reshape(shape), residual.reshape(shape)

    split = P("tm", None, "sx", "sy", None)
    return jax.shard_map(
        local,
        mesh=mesh,
        in_specs=(split, split, P(None, "sx", "sy", None), P(), P()),
        out_specs=(split, split),
        check_vma=False,
    )
```

```python
import functools

import jax
import jax.numpy as jnp
from jax import lax
from jax.experimental import pallas as pl
from jax.experimental.pallas import tpu as pltpu
from jax.sharding import PartitionSpec as P

MESH = pl.DeviceIdType.MESH
F32, BF16 = jnp.float32, jnp.bfloat16
STEPS = 4
LANES = 128


def halves(value):
    high = value.astype(BF16)
    return high, (value - high.astype(F32)).astype(BF16)


def kernel(
    counts, nx, ny,
    state_hbm, force_hbm, init_hbm, vol_hbm, lift_hbm,
    kept, resid, error,
    raw_start, raw_state, raw_force, volume, lift,
    fields, source, earlier,
    halo_x, halo_y, sent_y, stack, lows,
    load_sem, face_send, face_recv, start_send, start_recv, err_send, err_recv,
):
    n_tm, n_sx, n_sy = counts
    cells = nx * ny
    tm, sx, sy = lax.axis_index("tm"), lax.axis_index("sx"), lax.axis_index("sy")
    first, more = tm == 0, tm < n_tm - 1
    exists = (sx < n_sx - 1, sx > 0, sy < n_sy - 1, sy > 0)
    comes = (sx > 0, sx < n_sx - 1, sy > 0, sy < n_sy - 1)
    shifts = ((1, 0), (-1, 0), (0, 1), (0, -1))

    def place(dt, f):
        dx, dy = shifts[f]
        return {"tm": tm + dt, "sx": sx + dx, "sy": sy + dy}

    barrier = pltpu.get_barrier_semaphore()

    def greet(dt, f):
        pl.semaphore_signal(barrier, inc=1, device_id=place(dt, f), device_id_type=MESH)

    for f in range(4):
        pl.when(exists[f])(functools.partial(greet, 0, f))
        pl.when(exists[f] & (tm > 0))(functools.partial(greet, -1, f))

    @pl.when(tm > 0)
    def _():
        pl.semaphore_signal(
            barrier, inc=1, device_id={"tm": tm - 1, "sx": sx, "sy": sy}, device_id_type=MESH
        )

    load_state = pltpu.make_async_copy(state_hbm, raw_state, load_sem.at[0])
    load_force = pltpu.make_async_copy(force_hbm, raw_force, load_sem.at[1])
    load_init = pltpu.make_async_copy(init_hbm, raw_start, load_sem.at[2])

    @pl.when(first)
    def _():
        load_init.start()

    load_state.start()
    load_force.start()
    load_volume = pltpu.make_async_copy(vol_hbm, volume, load_sem.at[3])
    load_lift = pltpu.make_async_copy(lift_hbm, lift, load_sem.at[4])
    load_volume.start()
    load_lift.start()

    wide, tall = ny * LANES, cells * LANES
    for shift in (0, 96):
        stack[64 + shift : 80 + shift, 0:wide] = jnp.zeros((16, wide), BF16)
        stack[80 + shift : 96 + shift, tall - wide : tall] = jnp.zeros((16, wide), BF16)
        for x in range(nx):
            left, right = x * wide, (x + 1) * wide
            stack[96 + shift : 112 + shift, left : left + LANES] = jnp.zeros((16, LANES), BF16)
            stack[112 + shift : 128 + shift, right - LANES : right] = jnp.zeros((16, LANES), BF16)

    def no_halo(f):
        ref = (halo_x, halo_x, halo_y, halo_y)[f]
        for phase in range(STEPS + 1):
            ref[phase, f % 2] = jnp.zeros(ref.shape[2:], F32)

    for f in range(4):
        pl.when(jnp.logical_not(comes[f]))(functools.partial(no_halo, f))

    total = sum(e.astype(jnp.int32) for e in exists)
    pl.semaphore_wait(barrier, total + jnp.where(more, total + 1, 0))

    def start_copy(x):
        part = pl.ds(x * 64 * ny, 64 * ny)
        return pltpu.make_async_remote_copy(
            src_ref=state_hbm.at[part], dst_ref=raw_start.at[part],
            send_sem=start_send.at[x], recv_sem=start_recv.at[x],
            device_id={"tm": tm + 1, "sx": sx, "sy": sy}, device_id_type=MESH,
        )

    top = lax.broadcasted_iota(jnp.int32, (8, LANES), 0) < 4
    lane = lax.broadcasted_iota(jnp.int32, (16, LANES), 1)

    def y_plus(ref, cell):
        parts = []
        for p in range(0, 64, 32):
            one, two = ref[cell, p + 8 : p + 16, :], ref[cell, p + 24 : p + 32, :]
            parts.append(jnp.where(top, pltpu.roll(one, 4, 0), two))
        return jnp.concatenate(parts, axis=0)

    def y_minus(ref, cell):
        parts = []
        for p in range(0, 64, 32):
            one, two = ref[cell, p : p + 8, :], ref[cell, p + 16 : p + 24, :]
            parts.append(jnp.where(top, one, pltpu.roll(two, 4, 0)))
        return jnp.concatenate(parts, axis=0)

    def face_copy(ref, slot, phase, dt, f, to=None):
        if f == 0:
            src = ref.at[pl.ds(cells - ny, ny), pl.ds(48, 16), :]
        elif f == 1:
            src = ref.at[pl.ds(0, ny), pl.ds(0, 16), :]
        else:
            src = sent_y.at[slot, f - 2]
        target = (halo_x, halo_x, halo_y, halo_y)[f].at[phase, f % 2]
        return pltpu.make_async_remote_copy(
            src_ref=src, dst_ref=target,
            send_sem=face_send.at[dt, f], recv_sem=face_recv.at[phase, f],
            device_id=place(dt, f if to is None else to), device_id_type=MESH,
        )

    def send_faces(ref, slot, phase, dt):
        odd = lax.rem(sx, 2) == 1
        pl.when(exists[0] & odd)(face_copy(ref, slot, phase, dt, 0).start)
        pl.when(exists[1])(face_copy(ref, slot, phase, dt, 1).start)
        pl.when(exists[0] & jnp.logical_not(odd))(face_copy(ref, slot, phase, dt, 0).start)
        for x in range(nx):
            sent_y[slot, 0, x] = y_plus(ref, x * ny + ny - 1)
            sent_y[slot, 1, x] = y_minus(ref, x * ny)
        for f in range(2, 4):
            pl.when(exists[f])(face_copy(ref, slot, phase, dt, f).start)

    def sent_faces(dt, phases):
        for f in range(4):
            block = (halo_x, halo_x, halo_y, halo_y)[f].at[pl.ds(0, phases), f % 2]
            copy = pltpu.make_async_remote_copy(
                src_ref=block, dst_ref=block, send_sem=face_send.at[dt, f], recv_sem=face_recv.at[0, f],
                device_id=place(dt, f), device_id_type=MESH,
            )
            pl.when(exists[f])(copy.wait_send)

    def reorder(raw, ref):
        for cell in range(cells):
            ref[cell] = raw[pl.ds(cell, 64, stride=cells), :]

    def inside(ref, finish):
        def put(rows, cell, pair):
            cols = slice(cell * LANES, (cell + 1) * LANES)
            stack[rows : rows + 16, cols] = pair[0]
            stack[rows + 96 : rows + 112, cols] = pair[1]

        for x in range(nx):
            for y in range(ny):
                cell = x * ny + y
                high, low = halves(ref[cell])
                stack[0:64, cell * LANES : (cell + 1) * LANES] = high
                lows[x * 64 : (x + 1) * 64, y * LANES : (y + 1) * LANES] = low
                if x + 1 < nx:
                    put(64, cell + ny, (high[48:64], low[48:64]))
                if x > 0:
                    put(80, cell - ny, (high[0:16], low[0:16]))
                if y + 1 < ny:
                    put(96, cell + 1, halves(y_plus(ref, cell)))
                if y > 0:
                    put(112, cell - 1, halves(y_minus(ref, cell)))
                up = pltpu.roll(ref[cell, pl.ds(3, 16, stride=4), :], 1, 1)
                put(128, cell, halves(jnp.where(lane == 0, 0.0, up)))
                down = pltpu.roll(ref[cell, pl.ds(0, 16, stride=4), :], LANES - 1, 1)
                put(144, cell, halves(jnp.where(lane == LANES - 1, 0.0, down)))
        rest = jnp.dot(low_matrix, lows[...], preferred_element_type=F32)
        for x in range(nx):
            cols = slice(x * wide, (x + 1) * wide)
            both = jnp.dot(main_matrix, stack[:, cols], preferred_element_type=F32)
            delta = both[:64] + both[64:] + rest[x * 64 : (x + 1) * 64]
            for y in range(ny):
                finish(x * ny + y, delta[:, y * LANES : (y + 1) * LANES])

    def outside(phase, out, scale):
        for f in range(4):
            pl.when(comes[f])(face_copy(kept, STEPS + 1, phase, 0, f, f ^ 1).wait_recv)
        rows = []
        for f in range(4):
            ref = (halo_x, halo_x, halo_y, halo_y)[f]
            blocks = [ref[phase, f % 2, i] for i in range(ref.shape[2])]
            blocks += [jnp.zeros((16, LANES), F32)] * (max(nx, ny) - len(blocks))
            high, low = halves(jnp.concatenate(blocks, axis=1))
            rows += [high, low, high]
        more_delta = jnp.dot(
            face_matrix, jnp.concatenate(rows, axis=0), preferred_element_type=F32
        )
        if scale != 1.0:
            more_delta = scale * more_delta
        sums = {}
        for f in range(4):
            for i in range((ny, ny, nx, nx)[f]):
                cell = (i, cells - ny + i, i * ny, i * ny + ny - 1)[f]
                part = more_delta[f * 64 : (f + 1) * 64, i * LANES : (i + 1) * LANES]
                sums[cell] = sums[cell] + part if cell in sums else part
        for cell, part in sums.items():
            out[cell] = out[cell] + part

    @pl.when(first)
    def _():
        load_init.wait()
        reorder(raw_start, fields.at[0])
        send_faces(fields.at[0], 0, 0, 0)

    @pl.when(more)
    def _():
        for x in range(nx):
            start_copy(x).start()

    load_state.wait()
    reorder(raw_state, kept)

    @pl.when(more)
    def _():
        send_faces(kept, STEPS + 1, 0, 1)

    load_force.wait()
    reorder(raw_force, source)

    load_volume.wait()
    load_lift.wait()
    row = lax.broadcasted_iota(jnp.int32, (64, 64), 0)
    column = lax.broadcasted_iota(jnp.int32, (64, 64), 1)
    weight = volume[...] - jnp.where(row == column, 0.1, 0.0).astype(F32)
    lifts = jnp.concatenate([lift[f] for f in range(6)], axis=0).T
    high, low = (half.astype(F32) for half in halves(jnp.concatenate([weight, lifts], axis=1)))

    def diagonal(blocks):
        rows, cols = blocks[0].shape
        return jnp.concatenate(
            [
                jnp.concatenate(
                    [block if i == j else jnp.zeros((rows, cols), F32) for j in range(len(blocks))], axis=1
                )
                for i, block in enumerate(blocks)
            ],
            axis=0,
        ).astype(BF16)

    main_matrix = jnp.concatenate(
        [
            jnp.concatenate([high, high[:, 64:]], axis=1),
            jnp.concatenate([low, jnp.zeros((64, 96), F32)], axis=1),
        ],
        axis=0,
    ).astype(BF16)
    low_matrix = diagonal([high[:, :64]] * nx)
    faces = [slice(64 + 16 * f, 80 + 16 * f) for f in range(4)]
    face_matrix = diagonal(
        [jnp.concatenate([high[:, at], high[:, at], low[:, at]], axis=1) for at in faces]
    )

    @pl.when(jnp.logical_not(first))
    def _():
        for x in range(nx):
            start_copy(x).wait_recv()
        reorder(raw_start, fields.at[0])

    early = [(x * ny + 1, ny - 2) for x in range(1, nx - 1)] if ny > 2 else []
    marks = [0] + [edge for start, size in early for edge in (start, start + size)] + [cells]
    late = [(low, high - low) for low, high in zip(marks[::2], marks[1::2])]

    def err_copy(part, ref):
        at = pl.ds(*part)
        index = (early + late).index(part)
        return pltpu.make_async_remote_copy(
            src_ref=ref.at[at], dst_ref=earlier.at[at],
            send_sem=err_send.at[index], recv_sem=err_recv.at[index],
            device_id={"tm": tm + 1, "sx": sx, "sy": sy}, device_id_type=MESH,
        )

    def send_early(ref):
        @pl.when(more)
        def _():
            for part in early:
                err_copy(part, ref).start()

    def send_late(ref):
        @pl.when(more)
        def _():
            send_faces(ref, STEPS, STEPS, 1)
            for part in late:
                err_copy(part, ref).start()

    for step in range(STEPS):
        now = fields.at[step]
        last = step == STEPS - 1
        out = resid if last else fields.at[step + 1]
        if step > 0:
            send_faces(now, step, step, 0)

        def finish(cell, delta, now=now, out=out, last=last):
            value = now[cell] + delta + source[cell]
            out[cell] = value - kept[cell] if last else value

        inside(now, finish)
        if last:
            pl.when(first)(functools.partial(send_early, resid))
        outside(step, out, 1.0)

    @pl.when(first)
    def _():
        send_late(resid)
        for cell in range(cells):
            error[cell] = resid[cell]
        sent_faces(0, STEPS)

    @pl.when(jnp.logical_not(first))
    def _():
        sent_faces(0, STEPS - 1)
        for part in early + late:
            err_copy(part, error).wait_recv()

        def finish(cell, delta):
            error[cell] = resid[cell] + earlier[cell] + 4.0 * delta

        inside(earlier, finish)
        send_early(error)
        outside(STEPS, error, 4.0)
        send_late(error)

    @pl.when(more)
    def _():
        for x in range(nx):
            start_copy(x).wait_send()
        for part in early + late:
            err_copy(part, resid).wait_send()
        sent_faces(1, 2)


def finishing(nx, ny, kept, resid, error, corr_hbm, resid_hbm, out_c, out_r, out_sem):
    cells = nx * ny
    copies = []
    for part in range(4):
        low, rows = part * 16 * cells, 16 * cells
        for cell in range(cells):
            dofs = slice(part * 16, part * 16 + 16)
            value = resid[cell, dofs, :]
            out_r[pl.ds(low + cell, 16, stride=cells), :] = value
            out_c[pl.ds(low + cell, 16, stride=cells), :] = kept[cell, dofs, :] + error[cell, dofs, :]
        for i, (src, dst) in enumerate(((out_r, resid_hbm), (out_c, corr_hbm))):
            span = pl.ds(low, rows)
            copies.append(pltpu.make_async_copy(src.at[span], dst.at[span], out_sem.at[part, i]))
            copies[-1].start()
    for copy in copies:
        copy.wait()


def solution(mesh):
    counts = tuple(mesh.shape[axis] for axis in ("tm", "sx", "sy"))

    def local(slices_state, forcing, initial, volume, lift):
        _, dofs, nx, ny, nz = slices_state.shape
        cells = nx * ny
        rows = dofs * cells
        raw = pltpu.VMEM((rows, nz), F32)
        field = pltpu.VMEM((cells, dofs, nz), F32)
        flat = jax.ShapeDtypeStruct((rows, nz), F32)
        shaped = jax.ShapeDtypeStruct((cells, dofs, nz), F32)
        vmem, hbm = pl.BlockSpec(memory_space=pltpu.VMEM), pl.BlockSpec(memory_space=pltpu.HBM)
        parts = pl.pallas_call(
            functools.partial(kernel, counts, nx, ny),
            out_shape=(shaped,) * 3,
            in_specs=[hbm] * 5,
            out_specs=(vmem,) * 3,
            scratch_shapes=[
                raw, raw, raw, pltpu.VMEM(volume.shape, F32), pltpu.VMEM((6, 16, dofs), F32),
                pltpu.VMEM((STEPS, cells, dofs, nz), F32), field, field,
                pltpu.VMEM((STEPS + 1, 2, ny, 16, nz), F32),
                pltpu.VMEM((STEPS + 1, 2, nx, 16, nz), F32),
                pltpu.VMEM((STEPS + 2, 2, nx, 16, nz), F32),
                pltpu.VMEM((256, cells * nz), BF16), pltpu.VMEM((dofs * nx, ny * nz), BF16),
                pltpu.SemaphoreType.DMA((5,)),
                pltpu.SemaphoreType.DMA((2, 4)),
                pltpu.SemaphoreType.DMA((STEPS + 1, 4)),
                pltpu.SemaphoreType.DMA((nx,)),
                pltpu.SemaphoreType.DMA((nx,)),
                pltpu.SemaphoreType.DMA((2 * nx,)),
                pltpu.SemaphoreType.DMA((2 * nx,)),
            ],
            compiler_params=pltpu.CompilerParams(
                collective_id=0, has_side_effects=True, vmem_limit_bytes=32 * 2**20
            ),
            name="cycle",
        )(
            *(
                pltpu.with_memory_space_constraint(value, pltpu.HBM)
                for value in (
                    slices_state.reshape(rows, nz), forcing.reshape(rows, nz),
                    initial.reshape(rows, nz), volume, jnp.swapaxes(lift, 1, 2),
                )
            )
        )
        corrected, residual = pl.pallas_call(
            functools.partial(finishing, nx, ny),
            out_shape=(flat,) * 2,
            in_specs=[vmem] * 3,
            out_specs=(hbm,) * 2,
            scratch_shapes=[raw, raw, pltpu.SemaphoreType.DMA((4, 2))],
            compiler_params=pltpu.CompilerParams(vmem_limit_bytes=16 * 2**20),
            name="finishing",
        )(*parts)
        shape = slices_state.shape
        return corrected.reshape(shape), residual.reshape(shape)

    split = P("tm", None, "sx", "sy", None)
    return jax.shard_map(
        local,
        mesh=mesh,
        in_specs=(split, split, P(None, "sx", "sy", None), P(), P()),
        out_specs=(split, split),
        check_vma=False,
    )
```
